512 devices in a mesh: bx: 32 (over z, core), by: 16 (over y, x).
Axes of the slice: x: 4, y: 4, z: 16, core: 2. Of those that a mesh axis runs over, the one named last changes fastest.
Arguments:
- rhs: float32 [256, 128, 256], P('bx', 'by'), may hold values from -5 to 6.5
- acoef: float32 [256, 128, 256], P('bx', 'by'), may hold values from 0.02 to 0.4
- beta_x: float32 [256, 128, 256], P('bx', 'by'), may hold values from 0.5 to 2
- beta_y: float32 [256, 128, 256], P('bx', 'by'), may hold values from 0.5 to 2
- beta_z: float32 [256, 128, 256], P('bx', 'by'), may hold values from 0.5 to 2
Outputs:
- solution: float32 [256, 128, 256], P('bx', 'by')
The draws below stay inside these ranges and needn't reach their ends.
All inputs are finite; a program needn't handle non-finite values.
Results may differ from the reference program's by a relative error of at most 0.0001.
Values sent between devices are 32-bit elements; how exact they have to be, the bound alone decides.
A program may use at most 64 MiB of HBM per device.

```python
import math
import jax
import jax.numpy as jnp
from jax import lax

NZ = 256
LEVELS = 3
PRE = 3
POST = 3
COARSE = 8
NX = 256
NY = 128


def draw_rhs(key, part):
    key = jax.random.fold_in(key, 11)
    noise = jnp.clip(jax.random.normal(key, (NX, NY, NZ), jnp.float32), -5.0, 5.0)
    return noise


def shard_levels(stream_key, shape, cuts, low, top_value):
    gain, own = 1.0, jax.random.fold_in(stream_key, 6)
    for dim, parts in cuts:
        draws = jnp.exp(jax.random.uniform(jax.random.fold_in(own, dim), (parts,), jnp.float32, low / len(cuts), top_value / len(cuts)))
        gain = gain * jnp.repeat(draws, shape[dim] // parts).reshape([-1 if axis == dim else 1 for axis in range(len(shape))])
    return gain


def setup_inputs(seed: int = 0) -> dict:
    streams_of = jax.random.split(jax.random.key(seed), 6)
    rhs = draw_rhs(jax.random.fold_in(streams_of[5], 71), 0)
    acoef = jnp.clip(jnp.exp(math.log(0.4) - 2.9957323 * jax.random.uniform(streams_of[1], (NX, NY, NZ), jnp.float32) ** shard_levels(streams_of[1], (NX, NY, NZ), ((0, 32), (1, 16)), -0.2, 0.2)), 0.02, 0.4)
    beta_x = jnp.clip(jnp.exp(math.log(2.0) - 1.3862944 * jax.random.uniform(streams_of[2], (NX, NY, NZ), jnp.float32) ** shard_levels(streams_of[2], (NX, NY, NZ), ((0, 32), (1, 16)), -0.2, 0.2)), 0.5, 2.0)
    beta_y = jnp.clip(jnp.exp(math.log(2.0) - 1.3862944 * jax.random.uniform(streams_of[3], (NX, NY, NZ), jnp.float32) ** shard_levels(streams_of[3], (NX, NY, NZ), ((0, 32), (1, 16)), -0.2, 0.2)), 0.5, 2.0)
    beta_z = jnp.clip(jnp.exp(math.log(2.0) - 1.3862944 * jax.random.uniform(streams_of[4], (NX, NY, NZ), jnp.float32) ** shard_levels(streams_of[4], (NX, NY, NZ), ((0, 32), (1, 16)), -0.2, 0.2)), 0.5, 2.0)
    return {"rhs": rhs, "acoef": acoef, "beta_x": beta_x, "beta_y": beta_y, "beta_z": beta_z}


damping = 0.8


def restrict_cells(values):
    size_x, size_y, size_z = values.shape
    blocks = values.reshape(size_x // 2, 2, size_y // 2, 2, size_z // 2, 2)
    return blocks.sum(axis=(1, 3, 5)) * 0.125


def coarse_faces(beta, axis_no):
    size_x, size_y, size_z = beta.shape
    blocks = beta.reshape(size_x // 2, 2, size_y // 2, 2, size_z // 2, 2)
    if axis_no == 0:
        picked = blocks[:, 0, :, :, :, :].sum(axis=(2, 4))
    elif axis_no == 1:
        picked = blocks[:, :, :, 0, :, :].sum(axis=(1, 4))
    else:
        picked = blocks[:, :, :, :, :, 0].sum(axis=(1, 3))
    return picked * 0.0625


def prolong(values):
    size_x, size_y, size_z = values.shape
    spread = jnp.broadcast_to(values[:, None, :, None, :, None], (size_x, 2, size_y, 2, size_z, 2))
    return spread.reshape(2 * size_x, 2 * size_y, 2 * size_z)


def lower_of(values, axis_no):
    count = values.shape[axis_no]
    zero_plane = jnp.zeros_like(lax.slice_in_dim(values, 0, 1, axis=axis_no))
    return jnp.concatenate([zero_plane, lax.slice_in_dim(values, 0, count - 1, axis=axis_no)], axis=axis_no)


def upper_of(values, axis_no):
    count = values.shape[axis_no]
    zero_plane = jnp.zeros_like(lax.slice_in_dim(values, 0, 1, axis=axis_no))
    return jnp.concatenate([lax.slice_in_dim(values, 1, count, axis=axis_no), zero_plane], axis=axis_no)


def build(cell_coef, face_x, face_y, face_z):
    high_x = upper_of(face_x, 0)
    high_y = upper_of(face_y, 1)
    high_z = upper_of(face_z, 2)
    diag = cell_coef + face_x + high_x + face_y + high_y + face_z + high_z
    return (cell_coef, face_x, high_x, face_y, high_y, face_z, high_z, diag)


def apply_op(values, coeffs):
    result = coeffs[7] * values - coeffs[1] * lower_of(values, 0) - coeffs[2] * upper_of(values, 0)
    result = result - coeffs[3] * lower_of(values, 1) - coeffs[4] * upper_of(values, 1)
    result = result - coeffs[5] * lower_of(values, 2) - coeffs[6] * upper_of(values, 2)
    return result


def smooth(values, source, coeffs, sweeps):
    for sweep_no in range(sweeps):
        values = values + damping * (source - apply_op(values, coeffs)) / coeffs[7]
    return values


def reference(rhs, acoef, beta_x, beta_y, beta_z):
    source = rhs
    cell_coef, face_x, face_y, face_z = acoef, beta_x, beta_y, beta_z
    stored = []
    for level_no in range(LEVELS):
        coeffs = build(cell_coef, face_x, face_y, face_z)
        values = damping * source / coeffs[7]
        values = smooth(values, source, coeffs, PRE - 1)
        remains = source - apply_op(values, coeffs)
        stored.append((values, source, coeffs))
        source = restrict_cells(remains)
        cell_coef = restrict_cells(cell_coef)
        face_x = coarse_faces(face_x, 0)
        face_y = coarse_faces(face_y, 1)
        face_z = coarse_faces(face_z, 2)
    coeffs = build(cell_coef, face_x, face_y, face_z)
    values = damping * source / coeffs[7]
    values = smooth(values, source, coeffs, COARSE - 1)
    for level_no in reversed(range(LEVELS)):
        fine_values, fine_source, fine_coeffs = stored[level_no]
        values = fine_values + prolong(values)
        values = smooth(values, fine_source, fine_coeffs, POST)
    return values
```

```python
import functools

import jax
import jax.numpy as jnp
from jax import lax
from jax.experimental import pallas as pl
from jax.experimental.pallas import tpu as pltpu
from jax.sharding import PartitionSpec as P

MESH = pl.DeviceIdType.MESH
F32 = jnp.float32
COARSE = 8

H0, H1, H2, H3 = 3, 9, 6, 10
X0, X1, X2 = 8 + 2 * H0, 4 + 2 * H1, 2 + 2 * H2
SLOTS, GROUPS = 2 * H3 + 1, (2 * H3 + 4) // 4


def reach(offset, size, halo):
    if offset == 0:
        return 0, size
    near = size * (abs(offset) - 1)
    count = min(size, halo - near)
    if count <= 0:
        return 0, 0
    return (0, count) if offset > 0 else (size - count, count)


def gap(offset, size):
    return 0 if offset == 0 else size * (abs(offset) - 1) + 1


AROUND = [(a, b) for a in (-1, 0, 1) for b in (-1, 0, 1) if (a, b) != (0, 0)]
WIDE = [
    (a, b)
    for a in range(-3, 4)
    for b in range(-3, 4)
    if (a, b) != (0, 0) and gap(a, 4) + gap(b, 4) <= H1
]
ALONG_X = [a for a in range(-H3, H3 + 1) if a]
ALONG_Y = list(range(1, 16))
NEAR = [-3, -2, -1, 1, 2, 3]
PARTNERS = sorted(set(WIDE) | {(a, 0) for a in ALONG_X} | {(0, b if b <= 8 else b - 16) for b in ALONG_Y})


def lanes(shape=(8, 128)):
    return lax.broadcasted_iota(jnp.int32, shape, 1)


def rows(shape=(8, 128)):
    return lax.broadcasted_iota(jnp.int32, shape, 0)


def pick(tile, index, axis):
    return jnp.take_along_axis(tile, index, axis=axis, mode="promise_in_bounds")


def up(value):
    return pltpu.roll(value, value.shape[0] - 1, 0)


def down(value):
    return pltpu.roll(value, 1, 0)


def right(value):
    return pltpu.roll(value, 127, 1)


def left(value):
    return pltpu.roll(value, 1, 1)


def coarsen(planes, kind, lane_index=None):
    out = []
    for i in range(0, len(planes), 2):
        total = planes[i] if kind == "x" else planes[i] + planes[i + 1]
        if kind != "y":
            total = total + up(total)
        total = pick(total, lax.rem(2 * rows(), 8), 0)
        if lane_index is not None:
            if kind != "z":
                total = total + right(total)
            total = pick(total, lane_index, 1)
        out.append(total * (0.125 if kind == "c" else 0.0625))
    return out


def couplings(get, bx, by, bz, x):
    v = get(x)
    cy, cz = by(x), bz(x)
    total = bx(x) * get(x - 1) + bx(x + 1) * get(x + 1)
    total = total + cy * down(v) + up(cy * v)
    return v, total + cz * left(v) + right(cz * v)


class Copies:
    def __init__(self, place, send_sems, recv_sems, number):
        self.place, self.number = place, number
        self.send_sem, self.recv_sem = send_sems.at[number], recv_sems.at[number]
        self.count = 0

    def start(self, source, target, offset):
        pltpu.make_async_remote_copy(
            src_ref=source,
            dst_ref=target,
            send_sem=self.send_sem,
            recv_sem=self.recv_sem,
            device_id=self.place(offset),
            device_id_type=MESH,
        ).start()
        size = 1
        for dim in source.shape:
            size *= dim
        self.count += size // 128

    def _wait(self, sem, dummy):
        part = dummy.at[pl.ds(0, self.count)]
        pltpu.make_async_copy(part, part, sem).wait()

    def arrived(self, dummy):
        self._wait(self.recv_sem, dummy)

    def sent(self, dummy):
        self._wait(self.send_sem, dummy)


def kernel(nx, ny, rhs, acoef, beta_x, beta_y, beta_z, out,
           F0, A0, E0, HX, HY, D0, W0, VA, VB, VP,
           F1, W1, P1, Q1, G1, U1,
           F2, W2, FP, P2, Q2,
           R3, RC, PK, PC, F3, W3, P3, Q3,
           dummy, send_sems, recv_sems):
    ix, iy = lax.axis_index("bx"), lax.axis_index("by")

    def place(offset):
        return (lax.rem(ix + (offset[0] % nx), nx), lax.rem(iy + (offset[1] % ny), ny))

    def group(number):
        return Copies(place, send_sems, recv_sems, number)

    barrier = pltpu.get_barrier_semaphore()
    for offset in PARTNERS:
        pl.semaphore_signal(barrier, inc=1, device_id=place(offset), device_id_type=MESH)

    lane, row = lanes(), rows()
    even = lax.rem(2 * lane, 128)
    keep_x = jnp.where(ix == 0, 0.0, 1.0).astype(F32)
    keep_y = jnp.where(iy == 0, 0.0, 1.0).astype(F32)
    keep_rows = jnp.where(row == 0, keep_y, 1.0)
    E, O = pl.ds(0, 128), pl.ds(128, 128)

    def split(ref, x):
        low, high = ref[x, :, E], ref[x, :, O]
        return tuple(
            jnp.where(lane < 64, pick(low, even + odd, 1), pick(high, even + odd, 1)) for odd in (0, 1)
        )

    own = pl.ds(0, 8)
    for x in range(8):
        px = H0 + x
        f, a, bx, by, bz = (split(ref, x) for ref in (rhs, acoef, beta_x, beta_y, beta_z))
        for half, part in ((0, E), (1, O)):
            bxm = bx[half] * keep_x if x == 0 else bx[half]
            bym = by[half] * keep_rows
            extra = by[half] - bym
            if x == 0:
                extra = extra + (bx[half] - bxm)
            bzm = bz[half]
            if half == 0:
                bzm = jnp.where(lane == 0, 0.0, bzm)
                extra = extra + (bz[half] - bzm)
            F0[0, px, own, part] = f[half]
            F0[1, px, own, part] = a[half] + extra
            F0[2, px, own, part] = bxm
            F0[3, px, own, part] = bym
            F0[4, px, own, part] = bzm
            A0[x, :, part] = a[half]
            E0[x, :, part] = extra

    pl.semaphore_wait(barrier, len(PARTNERS))

    faces = group(0)
    faces.start(F0.at[2, H0, own], HX.at[:, :], (-1, 0))
    faces.start(F0.at[3, pl.ds(H0, 8), pl.ds(0, 1)], HY.at[:, pl.ds(0, 1)], (0, -1))
    halo = group(1)

    def span_x(offset, wide):
        if offset == 0:
            return pl.ds(H0, 8), pl.ds(H0, 8)
        if offset < 0:
            return pl.ds(H0, wide), pl.ds(H0 + 8, wide)
        return pl.ds(H0 + 8 - wide, wide), pl.ds(H0 - wide, wide)

    def span_y(offset, wide):
        if offset == 0:
            return pl.ds(0, 8), pl.ds(0, 8)
        if offset < 0:
            return pl.ds(0, wide), pl.ds(8, wide)
        return pl.ds(8 - wide, wide), pl.ds(16 - wide, wide)

    def spans(dx, dy):
        width = 2 if dx > 0 and dy > 0 else 3
        sx, tx = span_x(dx, width)
        sy, ty = span_y(dy, width)
        return sx, sy, tx, ty

    for dx, dy in AROUND:
        sx, sy, tx, ty = spans(dx, dy)
        halo.start(F0.at[:, sx, sy], F0.at[:, tx, ty], (dx, dy))
    halo.start(F0.at[2, H0 + 3, own], F0.at[2, H0 + 11, own], (-1, 0))
    halo.start(F0.at[3, pl.ds(H0, 8), pl.ds(3, 1)], F0.at[3, pl.ds(H0, 8), pl.ds(11, 1)], (0, -1))

    def both(get):
        return [get(x, E) + get(x, O) for x in range(8)]

    to64, to32 = even, lax.rem(2 * lane, 64)
    a1 = coarsen(both(lambda x, p: A0[x, :, p]), "c")
    e1 = [0.5 * t for t in coarsen(both(lambda x, p: E0[x, :, p]), "c")]
    bx1 = coarsen(both(lambda x, p: F0[2, H0 + x, own, p]), "x")
    by1 = coarsen(both(lambda x, p: F0[3, H0 + x, own, p]), "y")
    bz1 = coarsen([F0[4, H0 + x, own, E] for x in range(8)], "z")
    a2 = coarsen(a1, "c", to64)
    e2 = [0.5 * t for t in coarsen(e1, "c", to64)]
    bx2, by2, bz2 = coarsen(bx1, "x", to64), coarsen(by1, "y", to64), coarsen(bz1, "z", to64)
    a3 = coarsen(a2, "c", to32)
    e3 = [0.5 * t for t in coarsen(e2, "c", to32)]
    bx3, by3, bz3 = coarsen(bx2, "x", to32), coarsen(by2, "y", to32), coarsen(bz2, "z", to32)

    faces.arrived(dummy)
    hx = HX[:, E] + HX[:, O]
    hx1 = coarsen([hx, hx], "x")[0]
    hx2 = coarsen([hx1, hx1], "x", to64)[0]
    hx3 = coarsen([hx2, hx2], "x", to32)[0]
    hy = [HY[x, :, E] + HY[x, :, O] for x in range(8)]
    hy1 = [0.0625 * (hy[2 * i] + hy[2 * i + 1]) for i in range(4)]

    def squeeze(t, index):
        return pick(t + right(t), index, 1) * 0.0625

    hy2 = [squeeze(hy1[2 * i] + hy1[2 * i + 1], to64) for i in range(2)]
    hy3 = squeeze(hy2[0] + hy2[1], to32)

    def diag_of(a, e, bx, by, bz, hx_plane, hy_rows, last):
        result = []
        for i in range(len(a)):
            high_x = bx[i + 1] if i + 1 < len(a) else hx_plane
            edge = pltpu.roll(hy_rows[i], last, 0) if last else hy_rows[i]
            high_y = jnp.where(row == last, edge, up(by[i]))
            result.append(a[i] + e[i] + bx[i] + high_x + by[i] + high_y + bz[i] + right(bz[i]))
        return result

    d1 = diag_of(a1, e1, bx1, by1, bz1, hx1, hy1, 3)
    d2 = diag_of(a2, e2, bx2, by2, bz2, hx2, hy2, 1)
    d3 = diag_of(a3, e3, bx3, by3, bz3, hx3, [hy3], 0)
    for number, field in enumerate((d1, bx1, by1, bz1)):
        for i in range(4):
            F1[1 + number, H1 + i, pl.ds(0, 4)] = field[i][0:4]
    for number, field in enumerate((d2, bx2, by2, bz2)):
        for i in range(2):
            F2[2 + number, H2 + i, pl.ds(0, 2)] = field[i][0:2]
    for number, field in enumerate((d3, bx3, by3, bz3)):
        RC[number, H3] = field[0][0:1]

    def wide_spans(dx, dy):
        fx, cx = reach(-dx, 4, H1)
        fy, cy = reach(-dy, 4, H1)
        return pl.ds(H1 + fx, cx), pl.ds(fy, cy), pl.ds(H1 - 4 * dx + fx, cx), pl.ds((fy - 4 * dy) % 24, cy)

    wide = group(2)
    for dx, dy in WIDE:
        sx, sy, tx, ty = wide_spans(dx, dy)
        wide.start(F1.at[pl.ds(1, 4), sx, sy], F1.at[pl.ds(1, 4), tx, ty], (dx, dy))
    two = pl.ds(0, 2)
    mid = pl.ds(H2, 2)
    coef2x = group(3)
    for dx in NEAR:
        coef2x.start(F2.at[pl.ds(2, 4), mid, two], F2.at[pl.ds(2, 4), pl.ds(H2 - 2 * dx, 2), two], (dx, 0))
    coef3x = group(4)
    for dx in ALONG_X:
        coef3x.start(RC.at[:, H3], RC.at[:, H3 - dx], (dx, 0))

    halo.arrived(dummy)
    for x in range(X0):
        hz = F0[4, x, :, E], F0[4, x, :, O]
        for half, part in ((0, E), (1, O)):
            by = F0[3, x, :, part]
            total = F0[1, x, :, part] + F0[2, x, :, part] + F0[2, x + 1, :, part] + by + up(by) + hz[half]
            total = total + (hz[1] if half == 0 else right(hz[0]))
            w = 0.8 / total
            W0[x, :, part] = w
            VA[x, :, part] = w * F0[0, x, :, part]
            if H0 <= x < H0 + 8:
                D0[x - H0, :, part] = total[0:8]

    def couplings0(src, x, count=16):
        ve, vo = src[x, :, E], src[x, :, O]
        ze, zo = F0[4, x, :, E], F0[4, x, :, O]
        sums = []
        for v, part in ((ve, E), (vo, O)):
            by = F0[3, x, :, part]
            total = F0[2, x, :, part] * src[x - 1, :, part] + F0[2, x + 1, :, part] * src[x + 1, :, part]
            sums.append(total + by * down(v) + up(by * v))
        sums[0] = sums[0] + ze * left(vo) + zo * vo
        sums[1] = sums[1] + zo * ve + right(ze * ve)
        return ((ve, sums[0], E), (vo, sums[1], O))

    def sweep0(src, dst, first, last):
        for x in range(first, last):
            for v, total, part in couplings0(src, x):
                dst[x, :, part] = 0.2 * v + W0[x, :, part] * (F0[0, x, :, part] + total)

    sweep0(VA, VB, 1, X0 - 1)
    sweep0(VB, VA, 2, X0 - 2)
    remains = []
    for x in range(8):
        parts = []
        for v, total, part in couplings0(VA, H0 + x):
            v, total = v[0:8], total[0:8]
            parts.append(F0[0, H0 + x, own, part] + total - D0[x, :, part] * v)
            VP[H0 + x, own, part] = v
        remains.append(parts[0] + parts[1])
    f1 = coarsen(remains, "c")
    for i in range(4):
        F1[0, H1 + i, pl.ds(0, 4)] = f1[i][0:4]

    wide_f = group(5)
    for dx, dy in WIDE:
        sx, sy, tx, ty = wide_spans(dx, dy)
        wide_f.start(F1.at[0, sx, sy], F1.at[0, tx, ty], (dx, dy))
    halo_v = group(6)
    for dx, dy in AROUND:
        sx, sy, tx, ty = spans(dx, dy)
        halo_v.start(VP.at[sx, sy], VP.at[tx, ty], (dx, dy))

    every = pl.ds(0, X2)
    coef2x.arrived(dummy)
    coef2y = group(7)
    for dy in NEAR:
        target = pl.ds((-2 * dy) % 16, 2)
        coef2y.start(F2.at[pl.ds(2, 4), every, two], F2.at[pl.ds(2, 4), every, target], (0, dy))

    def packed(get):
        result = []
        for g in range(GROUPS):
            columns = [get(min(4 * g + k, SLOTS - 1)) for k in range(4)]
            line = lane[0:1]
            result.append(
                jnp.where(
                    line < 64,
                    jnp.where(line < 32, columns[0], columns[1]),
                    jnp.where(line < 96, columns[2], columns[3]),
                )
            )
        return result

    one = pl.ds(0, 1)
    coef3x.arrived(dummy)
    for number in range(4):
        for g, value in enumerate(packed(lambda s: RC[number, s])):
            PC[number, g, one] = value
            F3[1 + number, g, one] = value
    coef3y = group(8)
    for dy in ALONG_Y:
        coef3y.start(PC.at[:, :, one], F3.at[pl.ds(1, 4), :, pl.ds(16 - dy, 1)], (0, dy))

    wide.arrived(dummy)
    for x in range(X1):
        W1[x] = 0.8 / F1[1, x]
    coef2y.arrived(dummy)
    for x in range(X2):
        W2[x] = 0.8 / F2[2, x]

    def face(ref, number):
        return lambda x: ref[number, x]

    def sweep(src, dst, coeffs, source, weight, first, last, shift=0):
        for x in range(first, last):
            v, total = couplings(lambda p: src[p - shift], *coeffs, x)
            dst[x - shift] = 0.2 * v + weight[x] * (source(x) + total)

    c1 = face(F1, 2), face(F1, 3), face(F1, 4)
    wide_f.arrived(dummy)
    for x in range(X1):
        P1[x] = W1[x] * F1[0, x]
    sweep(P1, Q1, c1, face(F1, 0), W1, 1, X1 - 1)
    sweep(Q1, P1, c1, face(F1, 0), W1, 2, X1 - 2)

    def remains1(x):
        v, total = couplings(lambda p: P1[p], *c1, x)
        return F1[0, x] + total - F1[1, x] * v

    pairs = lax.rem(2 * row, 8)
    for i in range(8):
        x = H1 - 6 + 2 * i
        total = remains1(x) + remains1(x + 1)
        tiles = []
        for t in range(3):
            tile = total[8 * t : 8 * t + 8]
            tiles.append(pick(tile + up(tile), pairs, 0))
        tiles = [jnp.where(row < 4, tiles[0], tiles[1]), tiles[2]]
        tiles = [pick(tile + right(tile), to64, 1) * 0.125 for tile in tiles]
        FP[i] = jnp.concatenate(tiles, axis=0)

    c2 = face(F2, 3), face(F2, 4), face(F2, 5)
    for i in range(8):
        P2[i] = W2[i + 3] * FP[i]
    sweep(P2, Q2, c2, lambda x: FP[x - 3], W2, 4, 10, 3)
    sweep(Q2, P2, c2, lambda x: FP[x - 3], W2, 5, 9, 3)
    total = None
    for x in (6, 7):
        v, s = couplings(lambda p: P2[p - 3], *c2, x)
        rest = (FP[x - 3] + s - F2[2, x] * v)[0:8]
        total = rest if total is None else total + rest
        F2[0, x, two] = FP[x - 3][0:2]
        F2[1, x, two] = v[0:2]
    total = total + up(total)
    f3 = (pick(total + right(total), to32, 1) * 0.125)[0:1]
    R3[H3] = f3

    near3x = group(9)
    for dx in ALONG_X:
        near3x.start(R3.at[H3], R3.at[H3 - dx], (dx, 0))
    near2x = group(10)
    for dx in NEAR:
        near2x.start(F2.at[two, mid, two], F2.at[two, pl.ds(H2 - 2 * dx, 2), two], (dx, 0))

    for x in range(14):
        p = H1 - 5 + x
        for number, get in enumerate((face(F1, 0), lambda q: W1[q], face(F1, 2), face(F1, 3), face(F1, 4), lambda q: P1[q])):
            value = get(p)
            mixed = jnp.where(row < 3, value[8:16], value[16:24])
            G1[number, x] = jnp.concatenate([value[0:8], mixed], axis=0)
    coef3y.arrived(dummy)
    for g in range(GROUPS):
        W3[g] = 0.8 / F3[1, g]

    near3x.arrived(dummy)
    for g, value in enumerate(packed(lambda s: R3[s])):
        PK[g, one] = value
        F3[0, g, one] = value
    near3y = group(11)
    for dy in ALONG_Y:
        near3y.start(PK.at[:, one], F3.at[0, :, pl.ds(16 - dy, 1)], (0, dy))
    near2x.arrived(dummy)
    near2y = group(12)
    for dy in NEAR:
        target = pl.ds((-2 * dy) % 16, 2)
        near2y.start(F2.at[two, every, two], F2.at[two, every, target], (0, dy))
    halo_v.arrived(dummy)
    faces.sent(dummy)
    halo.sent(dummy)
    wide.sent(dummy)
    coef2x.sent(dummy)
    coef3x.sent(dummy)
    wide_f.sent(dummy)
    halo_v.sent(dummy)
    coef2y.sent(dummy)
    coef3y.sent(dummy)
    near3x.sent(dummy)
    near2x.sent(dummy)

    near3y.arrived(dummy)
    line = lanes((16, 128))
    for g in range(GROUPS):
        P3[g] = W3[g] * F3[0, g]
    src, dst = P3, Q3
    for step in range(COARSE - 1):
        for g in range(GROUPS):
            v, cx, cy, cz = src[g], F3[2, g], F3[3, g], F3[4, g]
            ahead = min(g + 1, GROUPS - 1)
            low = jnp.where(line < 32, pltpu.roll(src[max(g - 1, 0)], 32, 1), pltpu.roll(v, 32, 1))
            high = jnp.where(
                line >= 96, pltpu.roll(F3[2, ahead] * src[ahead], 96, 1), pltpu.roll(cx * v, 96, 1)
            )
            total = cx * low + high + cy * down(v) + up(cy * v) + cz * left(v) + right(cz * v)
            dst[g] = 0.2 * v + W3[g] * (F3[0, g] + total)
        src, dst = dst, src

    half_rows = lax.shift_right_logical(row, 1)

    def onto2(x):
        slot = H3 + x
        index = 32 * (slot % 4) + lax.shift_right_logical(lax.rem(lane, 64), 1)
        value = src[slot // 4]
        low, high = (pick(value[8 * t : 8 * t + 8], index, 1) for t in (0, 1))
        return jnp.concatenate([pick(low, half_rows, 0), pick(high, half_rows + 4, 0)], axis=0)

    lifted = [onto2(x) for x in range(-3, 4)]
    near2y.arrived(dummy)
    for x in range(X2):
        P2[x] = F2[1, x] + lifted[x // 2]
    sweep(P2, Q2, c2, face(F2, 0), W2, 1, X2 - 1)
    sweep(Q2, P2, c2, face(F2, 0), W2, 2, X2 - 2)
    sweep(P2, Q2, c2, face(F2, 0), W2, 3, X2 - 3)

    half_lanes = lax.shift_right_logical(lane, 1)

    def finer(value, limit, lane_index=None):
        tiles = [value[0:8], value[8:16]]
        if lane_index is not None:
            tiles = [pick(tile, lane_index, 1) for tile in tiles]
        upper = jnp.where(row < limit, pick(tiles[0], half_rows + 4, 0), pick(tiles[1], half_rows + 4, 0))
        return jnp.concatenate([pick(tiles[0], half_rows, 0), upper], axis=0)

    lifted = [finer(Q2[H2 + x], 3, half_lanes) for x in range(-3, 5)]
    for x in range(14):
        P1_16 = G1[5, x] + lifted[(x - 5) // 2 + 3]
        U1[0, x] = P1_16
    g1 = face(G1, 2), face(G1, 3), face(G1, 4)
    even_v, odd_v = U1.at[0], U1.at[1]
    weight1 = G1.at[1]
    sweep(even_v, odd_v, g1, face(G1, 0), weight1, 1, 13)
    sweep(odd_v, even_v, g1, face(G1, 0), weight1, 2, 12)
    sweep(even_v, odd_v, g1, face(G1, 0), weight1, 3, 11)

    lifted = [finer(odd_v[5 + x], 4) for x in range(-2, 6)]
    for x in range(X0):
        for part in (E, O):
            VA[x, :, part] = VP[x, :, part] + lifted[(x - 3) // 2 + 2]
    sweep0(VA, VB, 1, X0 - 1)
    sweep0(VB, VA, 2, X0 - 2)
    is_even = lax.rem(lane, 2) == 0
    for x in range(8):
        halves = []
        for v, total, part in couplings0(VA, H0 + x):
            result = 0.2 * v[0:8] + W0[H0 + x, own, part] * (F0[0, H0 + x, own, part] + total[0:8])
            halves.append(result)
        for part, index in ((E, half_lanes), (O, half_lanes + 64)):
            out[x, :, part] = jnp.where(is_even, pick(halves[0], index, 1), pick(halves[1], index, 1))

    near3y.sent(dummy)
    near2y.sent(dummy)


def solution(mesh):
    nx, ny = mesh.shape["bx"], mesh.shape["by"]

    def vmem(*shape):
        return pltpu.VMEM(shape, F32)

    def body(*args):
        return pl.pallas_call(
            functools.partial(kernel, nx, ny),
            out_shape=jax.ShapeDtypeStruct((8, 8, 256), F32),
            in_specs=[pl.BlockSpec(memory_space=pltpu.VMEM)] * 5,
            out_specs=pl.BlockSpec(memory_space=pltpu.VMEM),
            scratch_shapes=[
                vmem(5, X0 + 1, 16, 256), vmem(8, 8, 256), vmem(8, 8, 256), vmem(8, 256), vmem(8, 8, 256),
                vmem(8, 8, 256), vmem(X0, 16, 256), vmem(X0, 16, 256), vmem(X0, 16, 256), vmem(X0, 16, 256),
                vmem(5, X1 + 1, 24, 128), vmem(X1, 24, 128), vmem(X1, 24, 128), vmem(X1, 24, 128),
                vmem(6, 14, 16, 128), vmem(2, 14, 16, 128),
                vmem(6, X2, 16, 128), vmem(X2, 16, 128), vmem(8, 16, 128), vmem(X2, 16, 128), vmem(X2, 16, 128),
                vmem(SLOTS, 1, 128), vmem(4, SLOTS, 1, 128), vmem(GROUPS, 8, 128), vmem(4, GROUPS, 8, 128),
                vmem(5, GROUPS, 16, 128), vmem(GROUPS, 16, 128), vmem(GROUPS, 16, 128), vmem(GROUPS, 16, 128),
                vmem(8192, 128),
                pltpu.SemaphoreType.DMA((13,)), pltpu.SemaphoreType.DMA((13,)),
            ],
            compiler_params=pltpu.CompilerParams(
                collective_id=0, has_side_effects=True, vmem_limit_bytes=40 * 2**20
            ),
        )(*args)

    return jax.shard_map(
        body,
        mesh=mesh,
        in_specs=(P("bx", "by", None),) * 5,
        out_specs=P("bx", "by", None),
        check_vma=False,
    )
```

```python
import functools

import jax
import jax.numpy as jnp
from jax import lax
from jax.experimental import pallas as pl
from jax.experimental.pallas import tpu as pltpu
from jax.sharding import PartitionSpec as P

MESH = pl.DeviceIdType.MESH
F32 = jnp.float32
COARSE = 8

H0, H1, H2, H3 = 3, 9, 6, 10
X0, X1, X2 = 8 + 2 * H0, 4 + 2 * H1, 2 + 2 * H2
SLOTS, GROUPS = 2 * H3 + 1, (2 * H3 + 4) // 4


def reach(offset, size, halo):
    if offset == 0:
        return 0, size
    near = size * (abs(offset) - 1)
    count = min(size, halo - near)
    if count <= 0:
        return 0, 0
    return (0, count) if offset > 0 else (size - count, count)


def gap(offset, size):
    return 0 if offset == 0 else size * (abs(offset) - 1) + 1


AROUND = [(a, b) for a in (-1, 0, 1) for b in (-1, 0, 1) if (a, b) != (0, 0)]
WIDE = [
    (a, b)
    for a in range(-3, 4)
    for b in range(-3, 4)
    if (a, b) != (0, 0) and gap(a, 4) + gap(b, 4) <= H1
]
ALONG_X = [a for a in range(-H3, H3 + 1) if a]
ALONG_Y = list(range(1, 16))
NEAR = [-3, -2, -1, 1, 2, 3]
PARTNERS = sorted(set(WIDE) | {(a, 0) for a in ALONG_X} | {(0, b if b <= 8 else b - 16) for b in ALONG_Y})


def lanes(shape=(8, 128)):
    return lax.broadcasted_iota(jnp.int32, shape, 1)


def rows(shape=(8, 128)):
    return lax.broadcasted_iota(jnp.int32, shape, 0)


def pick(tile, index, axis):
    return jnp.take_along_axis(tile, index, axis=axis, mode="promise_in_bounds")


def up(value):
    return pltpu.roll(value, value.shape[0] - 1, 0)


def down(value):
    return pltpu.roll(value, 1, 0)


def right(value):
    return pltpu.roll(value, 127, 1)


def left(value):
    return pltpu.roll(value, 1, 1)


def coarsen(planes, kind, lane_index=None):
    out = []
    for i in range(0, len(planes), 2):
        total = planes[i] if kind == "x" else planes[i] + planes[i + 1]
        if kind != "y":
            total = total + up(total)
        total = pick(total, lax.rem(2 * rows(), 8), 0)
        if lane_index is not None:
            if kind != "z":
                total = total + right(total)
            total = pick(total, lane_index, 1)
        out.append(total * (0.125 if kind == "c" else 0.0625))
    return out


def couplings(get, bx, by, bz, x):
    v = get(x)
    cy, cz = by(x), bz(x)
    total = bx(x) * get(x - 1) + bx(x + 1) * get(x + 1)
    total = total + cy * down(v) + up(cy * v)
    return v, total + cz * left(v) + right(cz * v)


class Copies:
    def __init__(self, place, send_sems, recv_sems, number):
        self.place, self.number = place, number
        self.send_sem, self.recv_sem = send_sems.at[number], recv_sems.at[number]
        self.count = 0

    def start(self, source, target, offset):
        pltpu.make_async_remote_copy(
            src_ref=source,
            dst_ref=target,
            send_sem=self.send_sem,
            recv_sem=self.recv_sem,
            device_id=self.place(offset),
            device_id_type=MESH,
        ).start()
        size = 1
        for dim in source.shape:
            size *= dim
        self.count += size // 128

    def _wait(self, sem, dummy):
        part = dummy.at[pl.ds(0, self.count)]
        pltpu.make_async_copy(part, part, sem).wait()

    def arrived(self, dummy):
        self._wait(self.recv_sem, dummy)

    def sent(self, dummy):
        self._wait(self.send_sem, dummy)


def kernel(nx, ny, rhs, acoef, beta_x, beta_y, beta_z, out,
           IN, in_sems, F0, A0, E0, HX, HY, D0, W0, VA, VB, VP,
           F1, W1, P1, Q1, G1, U1,
           F2, S2, T2, W2, FP, P2, Q2,
           R3, RC, PK, PC, F3, W3, P3, Q3,
           dummy, send_sems, recv_sems):
    ix, iy = lax.axis_index("bx"), lax.axis_index("by")
    loads = [
        pltpu.make_async_copy(ref, IN.at[number], in_sems.at[number])
        for number, ref in enumerate((beta_x, beta_y, beta_z, acoef, rhs))
    ]
    for load in loads:
        load.start()

    def place(offset):
        return (lax.rem(ix + (offset[0] % nx), nx), lax.rem(iy + (offset[1] % ny), ny))

    def group(number):
        return Copies(place, send_sems, recv_sems, number)

    barrier = pltpu.get_barrier_semaphore()
    for offset in PARTNERS:
        pl.semaphore_signal(barrier, inc=1, device_id=place(offset), device_id_type=MESH)

    lane, row = lanes(), rows()
    even = lax.rem(2 * lane, 128)
    keep_x = jnp.where(ix == 0, 0.0, 1.0).astype(F32)
    keep_y = jnp.where(iy == 0, 0.0, 1.0).astype(F32)
    keep_rows = jnp.where(row == 0, keep_y, 1.0)
    E, O = pl.ds(0, 128), pl.ds(128, 128)

    def split(number, x):
        low, high = IN[number, x, :, E], IN[number, x, :, O]
        return tuple(
            jnp.where(lane < 64, pick(low, even + odd, 1), pick(high, even + odd, 1)) for odd in (0, 1)
        )

    own = pl.ds(0, 8)
    for load in loads:
        load.wait()
    for x in range(8):
        px = H0 + x
        bx, by, bz, a, f = (split(number, x) for number in range(5))
        for half, part in ((0, E), (1, O)):
            bxm = bx[half] * keep_x if x == 0 else bx[half]
            bym = by[half] * keep_rows
            extra = by[half] - bym
            if x == 0:
                extra = extra + (bx[half] - bxm)
            bzm = bz[half]
            if half == 0:
                bzm = jnp.where(lane == 0, 0.0, bzm)
                extra = extra + (bz[half] - bzm)
            F0[0, px, own, part] = f[half]
            F0[1, px, own, part] = a[half] + extra
            F0[2, px, own, part] = bxm
            F0[3, px, own, part] = bym
            F0[4, px, own, part] = bzm
            A0[x, :, part] = a[half]
            E0[x, :, part] = extra

    pl.semaphore_wait(barrier, len(PARTNERS))

    faces = group(0)
    faces.start(F0.at[2, H0, own], HX.at[:, :], (-1, 0))
    faces.start(F0.at[3, pl.ds(H0, 8), pl.ds(0, 1)], HY.at[:, pl.ds(0, 1)], (0, -1))
    halo = group(1)

    def span_x(offset, wide):
        if offset == 0:
            return pl.ds(H0, 8), pl.ds(H0, 8)
        if offset < 0:
            return pl.ds(H0, wide), pl.ds(H0 + 8, wide)
        return pl.ds(H0 + 8 - wide, wide), pl.ds(H0 - wide, wide)

    def span_y(offset, wide):
        if offset == 0:
            return pl.ds(0, 8), pl.ds(0, 8)
        if offset < 0:
            return pl.ds(0, wide), pl.ds(8, wide)
        return pl.ds(8 - wide, wide), pl.ds(16 - wide, wide)

    def spans(dx, dy):
        width = 2 if dx != 0 and dy != 0 else 3
        sx, tx = span_x(dx, width)
        sy, ty = span_y(dy, width)
        return sx, sy, tx, ty

    for dx, dy in AROUND:
        sx, sy, tx, ty = spans(dx, dy)
        halo.start(F0.at[:, sx, sy], F0.at[:, tx, ty], (dx, dy))
    halo.start(F0.at[2, H0 + 3, own], F0.at[2, H0 + 11, own], (-1, 0))
    halo.start(F0.at[3, pl.ds(H0, 8), pl.ds(3, 1)], F0.at[3, pl.ds(H0, 8), pl.ds(11, 1)], (0, -1))
    for dx, dy, number, x, y in (
        (-1, -1, 2, 2, 0), (-1, -1, 3, 2, 0), (-1, -1, 2, 0, 2), (-1, -1, 3, 0, 2),
        (-1, 1, 2, 2, 7), (-1, 1, 2, 0, 5), (1, -1, 3, 7, 2), (1, -1, 3, 5, 0),
    ):
        source = F0.at[number, H0 + x, pl.ds(y, 1)]
        halo.start(source, F0.at[number, H0 + x - 8 * dx, pl.ds((y - 8 * dy) % 16, 1)], (dx, dy))

    def both(get):
        return [get(x, E) + get(x, O) for x in range(8)]

    to64, to32 = even, lax.rem(2 * lane, 64)
    a1 = coarsen(both(lambda x, p: A0[x, :, p]), "c")
    e1 = [0.5 * t for t in coarsen(both(lambda x, p: E0[x, :, p]), "c")]
    bx1 = coarsen(both(lambda x, p: F0[2, H0 + x, own, p]), "x")
    by1 = coarsen(both(lambda x, p: F0[3, H0 + x, own, p]), "y")
    bz1 = coarsen([F0[4, H0 + x, own, E] for x in range(8)], "z")
    a2 = coarsen(a1, "c", to64)
    e2 = [0.5 * t for t in coarsen(e1, "c", to64)]
    bx2, by2, bz2 = coarsen(bx1, "x", to64), coarsen(by1, "y", to64), coarsen(bz1, "z", to64)
    a3 = coarsen(a2, "c", to32)
    e3 = [0.5 * t for t in coarsen(e2, "c", to32)]
    bx3, by3, bz3 = coarsen(bx2, "x", to32), coarsen(by2, "y", to32), coarsen(bz2, "z", to32)

    for number, field in enumerate((bx1, by1, bz1)):
        for i in range(4):
            F1[2 + number, H1 + i, pl.ds(0, 4)] = field[i][0:4]

    def wide_spans(dx, dy):
        fx, cx = reach(-dx, 4, H1)
        fy, cy = reach(-dy, 4, H1)
        return pl.ds(H1 + fx, cx), pl.ds(fy, cy), pl.ds(H1 - 4 * dx + fx, cx), pl.ds((fy - 4 * dy) % 24, cy)

    def send1(numbers, offset, collection):
        sx, sy, tx, ty = wide_spans(*offset)
        collection.start(F1.at[numbers, sx, sy], F1.at[numbers, tx, ty], offset)

    faces1y = group(2)
    for dy in NEAR:
        send1(pl.ds(2, 3), (0, dy), faces1y)

    faces.arrived(dummy)
    hx = HX[:, E] + HX[:, O]
    hx1 = coarsen([hx, hx], "x")[0]
    hx2 = coarsen([hx1, hx1], "x", to64)[0]
    hx3 = coarsen([hx2, hx2], "x", to32)[0]
    hy = [HY[x, :, E] + HY[x, :, O] for x in range(8)]
    hy1 = [0.0625 * (hy[2 * i] + hy[2 * i + 1]) for i in range(4)]

    def squeeze(t, index):
        return pick(t + right(t), index, 1) * 0.0625

    hy2 = [squeeze(hy1[2 * i] + hy1[2 * i + 1], to64) for i in range(2)]
    hy3 = squeeze(hy2[0] + hy2[1], to32)

    def diag_of(a, e, bx, by, bz, hx_plane, hy_rows, last):
        result = []
        for i in range(len(a)):
            high_x = bx[i + 1] if i + 1 < len(a) else hx_plane
            edge = pltpu.roll(hy_rows[i], last, 0) if last else hy_rows[i]
            high_y = jnp.where(row == last, edge, up(by[i]))
            result.append(a[i] + e[i] + bx[i] + high_x + by[i] + high_y + bz[i] + right(bz[i]))
        return result

    d1 = diag_of(a1, e1, bx1, by1, bz1, hx1, hy1, 3)
    d2 = diag_of(a2, e2, bx2, by2, bz2, hx2, hy2, 1)
    d3 = diag_of(a3, e3, bx3, by3, bz3, hx3, [hy3], 0)
    for i in range(4):
        F1[1, H1 + i, pl.ds(0, 4)] = d1[i][0:4]
    two = pl.ds(0, 2)
    mid = pl.ds(H2, 2)
    for i in range(2):
        own2 = [jnp.where(lane < 64, a, b) for a, b in ((d2[i], bx2[i]), (by2[i], bz2[i]))]
        for number in range(2):
            S2[number, H2 + i, two] = own2[number][0:2]
    for number, field in enumerate((d3, bx3, by3, bz3)):
        RC[number, H3] = field[0][0:1]

    diag1y = group(3)
    for dy in NEAR:
        send1(pl.ds(1, 1), (0, dy), diag1y)
    coef1x = group(4)
    for dx in NEAR:
        send1(pl.ds(1, 4), (dx, 0), coef1x)
    coef2y = group(6)
    for dy in NEAR:
        coef2y.start(S2.at[:, mid, two], S2.at[:, mid, pl.ds((-2 * dy) % 16, 2)], (0, dy))
    coef3x = group(8)
    for dx in ALONG_X:
        coef3x.start(RC.at[:, H3], RC.at[:, H3 - dx], (dx, 0))

    halo.arrived(dummy)
    for x in range(X0):
        hz = F0[4, x, :, E], F0[4, x, :, O]
        for half, part in ((0, E), (1, O)):
            by = F0[3, x, :, part]
            total = F0[1, x, :, part] + F0[2, x, :, part] + F0[2, x + 1, :, part] + by + up(by) + hz[half]
            total = total + (hz[1] if half == 0 else right(hz[0]))
            w = 0.8 / total
            W0[x, :, part] = w
            VA[x, :, part] = w * F0[0, x, :, part]
            if H0 <= x < H0 + 8:
                D0[x - H0, :, part] = total[0:8]

    def couplings0(src, x, count=16):
        ve, vo = src[x, :, E], src[x, :, O]
        ze, zo = F0[4, x, :, E], F0[4, x, :, O]
        sums = []
        for v, part in ((ve, E), (vo, O)):
            by = F0[3, x, :, part]
            total = F0[2, x, :, part] * src[x - 1, :, part] + F0[2, x + 1, :, part] * src[x + 1, :, part]
            sums.append(total + by * down(v) + up(by * v))
        sums[0] = sums[0] + ze * left(vo) + zo * vo
        sums[1] = sums[1] + zo * ve + right(ze * ve)
        return ((ve, sums[0], E), (vo, sums[1], O))

    def sweep0(src, dst, first, last):
        for x in range(first, last):
            for v, total, part in couplings0(src, x):
                dst[x, :, part] = 0.2 * v + W0[x, :, part] * (F0[0, x, :, part] + total)

    sweep0(VA, VB, 1, X0 - 1)
    sweep0(VB, VA, 2, X0 - 2)
    remains = []
    for x in range(8):
        parts = []
        for v, total, part in couplings0(VA, H0 + x):
            v, total = v[0:8], total[0:8]
            parts.append(F0[0, H0 + x, own, part] + total - D0[x, :, part] * v)
            VP[H0 + x, own, part] = v
        remains.append(parts[0] + parts[1])
    f1 = coarsen(remains, "c")
    for i in range(4):
        F1[0, H1 + i, pl.ds(0, 4)] = f1[i][0:4]

    wide_f = group(9)
    for offset in WIDE:
        sx, sy, tx, ty = wide_spans(*offset)
        wide_f.start(F1.at[0, sx, sy], F1.at[0, tx, ty], offset)

    faces1y.arrived(dummy)
    diag1y.arrived(dummy)
    corner1x = group(5)
    for dx in (-2, -1, 1, 2):
        fx, cx = reach(-dx, 4, H1)
        for first, count in ((4, 4), (20, 4)) if abs(dx) == 2 else ((4, 4), (8, 4), (16, 8)):
            span = pl.ds(first, count)
            corner1x.start(
                F1.at[pl.ds(1, 4), pl.ds(H1 + fx, cx), span],
                F1.at[pl.ds(1, 4), pl.ds(H1 - 4 * dx + fx, cx), span],
                (dx, 0),
            )

    def along_x2(collection, ref, lead):
        for dx in NEAR:
            for first, count in {1: ((0, 8), (10, 6)), 2: ((0, 5), (13, 3)), 3: ((0, 3), (15, 1))}[abs(dx)]:
                source = ref.at[(*lead, mid, pl.ds(first, count))]
                collection.start(source, ref.at[(*lead, pl.ds(H2 - 2 * dx, 2), pl.ds(first, count))], (dx, 0))

    coef2y.arrived(dummy)
    coef2x = group(7)
    along_x2(coef2x, S2, (slice(None),))

    def packed(get):
        result = []
        for g in range(GROUPS):
            columns = [get(min(4 * g + k, SLOTS - 1)) for k in range(4)]
            line = lane[0:1]
            result.append(
                jnp.where(
                    line < 64,
                    jnp.where(line < 32, columns[0], columns[1]),
                    jnp.where(line < 96, columns[2], columns[3]),
                )
            )
        return result

    one = pl.ds(0, 1)
    coef3x.arrived(dummy)
    for number in range(4):
        for g, value in enumerate(packed(lambda s: RC[number, s])):
            PC[number, g, one] = value
            F3[1 + number, g, one] = value
    coef1x.arrived(dummy)
    corner1x.arrived(dummy)
    for x in range(X1):
        W1[x] = 0.8 / F1[1, x]
    coef2x.arrived(dummy)
    wide_lanes = lanes((16, 128))

    def unpacked(value):
        swapped = pltpu.roll(value, 64, 1)
        return jnp.where(wide_lanes < 64, value, swapped), jnp.where(wide_lanes < 64, swapped, value)

    for x in range(X2):
        F2[2, x], F2[3, x] = unpacked(S2[0, x])
        F2[4, x], F2[5, x] = unpacked(S2[1, x])
        W2[x] = 0.8 / F2[2, x]

    def face(ref, number):
        return lambda x: ref[number, x]

    def sweep(src, dst, coeffs, source, weight, first, last, shift=0):
        for x in range(first, last):
            v, total = couplings(lambda p: src[p - shift], *coeffs, x)
            dst[x - shift] = 0.2 * v + weight[x] * (source(x) + total)

    c1 = face(F1, 2), face(F1, 3), face(F1, 4)
    wide_f.arrived(dummy)
    for x in range(X1):
        P1[x] = W1[x] * F1[0, x]
    sweep(P1, Q1, c1, face(F1, 0), W1, 1, X1 - 1)
    sweep(Q1, P1, c1, face(F1, 0), W1, 2, X1 - 2)

    def remains1(x):
        v, total = couplings(lambda p: P1[p], *c1, x)
        return F1[0, x] + total - F1[1, x] * v

    pairs = lax.rem(2 * row, 8)
    for i in range(8):
        x = H1 - 6 + 2 * i
        total = remains1(x) + remains1(x + 1)
        tiles = []
        for t in range(3):
            tile = total[8 * t : 8 * t + 8]
            tiles.append(pick(tile + up(tile), pairs, 0))
        tiles = [jnp.where(row < 4, tiles[0], tiles[1]), tiles[2]]
        tiles = [pick(tile + right(tile), to64, 1) * 0.125 for tile in tiles]
        FP[i] = jnp.concatenate(tiles, axis=0)

    c2 = face(F2, 3), face(F2, 4), face(F2, 5)
    for i in range(8):
        P2[i] = W2[i + 3] * FP[i]
    sweep(P2, Q2, c2, lambda x: FP[x - 3], W2, 4, 10, 3)
    sweep(Q2, P2, c2, lambda x: FP[x - 3], W2, 5, 9, 3)
    total = None
    for x in (6, 7):
        v, s = couplings(lambda p: P2[p - 3], *c2, x)
        rest = (FP[x - 3] + s - F2[2, x] * v)[0:8]
        total = rest if total is None else total + rest
        T2[x, two] = jnp.where(lane < 64, FP[x - 3][0:8], v[0:8])[0:2]
    total = total + up(total)
    f3 = (pick(total + right(total), to32, 1) * 0.125)[0:1]
    R3[H3] = f3

    near3x = group(10)
    for dx in ALONG_X:
        near3x.start(R3.at[H3], R3.at[H3 - dx], (dx, 0))
    near2y = group(11)
    for dy in NEAR:
        near2y.start(T2.at[mid, two], T2.at[mid, pl.ds((-2 * dy) % 16, 2)], (0, dy))
    coef3y = group(13)
    for dy in ALONG_Y:
        coef3y.start(PC.at[:, :, one], F3.at[pl.ds(1, 4), :, pl.ds(16 - dy, 1)], (0, dy))
    halo_v = group(12)
    for dx, dy in AROUND:
        sx, sy, tx, ty = spans(dx, dy)
        halo_v.start(VP.at[sx, sy], VP.at[tx, ty], (dx, dy))

    for x in range(14):
        p = H1 - 5 + x
        for number, get in enumerate((face(F1, 0), lambda q: W1[q], face(F1, 2), face(F1, 3), face(F1, 4), lambda q: P1[q])):
            value = get(p)
            mixed = jnp.where(row < 3, value[8:16], value[16:24])
            G1[number, x] = jnp.concatenate([value[0:8], mixed], axis=0)
    near3x.arrived(dummy)
    for g, value in enumerate(packed(lambda s: R3[s])):
        PK[g, one] = value
        F3[0, g, one] = value
    near3y = group(14)
    for dy in ALONG_Y:
        near3y.start(PK.at[:, one], F3.at[0, :, pl.ds(16 - dy, 1)], (0, dy))
    near2y.arrived(dummy)
    near2x = group(15)
    along_x2(near2x, T2, ())
    coef3y.arrived(dummy)
    for g in range(GROUPS):
        W3[g] = 0.8 / F3[1, g]
    halo_v.arrived(dummy)
    for done in (faces, halo, faces1y, diag1y, coef1x, coef2y, coef3x, wide_f, corner1x, coef2x, near3x, near2y, coef3y, halo_v):
        done.sent(dummy)

    near3y.arrived(dummy)
    line = lanes((16, 128))
    for g in range(GROUPS):
        P3[g] = W3[g] * F3[0, g]
    src, dst = P3, Q3
    for step in range(COARSE - 1):
        for g in range(GROUPS):
            v, cx, cy, cz = src[g], F3[2, g], F3[3, g], F3[4, g]
            ahead = min(g + 1, GROUPS - 1)
            low = jnp.where(line < 32, pltpu.roll(src[max(g - 1, 0)], 32, 1), pltpu.roll(v, 32, 1))
            high = jnp.where(
                line >= 96, pltpu.roll(F3[2, ahead] * src[ahead], 96, 1), pltpu.roll(cx * v, 96, 1)
            )
            total = cx * low + high + cy * down(v) + up(cy * v) + cz * left(v) + right(cz * v)
            dst[g] = 0.2 * v + W3[g] * (F3[0, g] + total)
        src, dst = dst, src

    half_rows = lax.shift_right_logical(row, 1)

    def onto2(x):
        slot = H3 + x
        index = 32 * (slot % 4) + lax.shift_right_logical(lax.rem(lane, 64), 1)
        value = src[slot // 4]
        low, high = (pick(value[8 * t : 8 * t + 8], index, 1) for t in (0, 1))
        return jnp.concatenate([pick(low, half_rows, 0), pick(high, half_rows + 4, 0)], axis=0)

    lifted = [onto2(x) for x in range(-3, 4)]
    near2x.arrived(dummy)
    for x in range(X2):
        F2[0, x], value = unpacked(T2[x])
        P2[x] = value + lifted[x // 2]
    sweep(P2, Q2, c2, face(F2, 0), W2, 1, X2 - 1)
    sweep(Q2, P2, c2, face(F2, 0), W2, 2, X2 - 2)
    sweep(P2, Q2, c2, face(F2, 0), W2, 3, X2 - 3)

    half_lanes = lax.shift_right_logical(lane, 1)

    def finer(value, limit, lane_index=None):
        tiles = [value[0:8], value[8:16]]
        if lane_index is not None:
            tiles = [pick(tile, lane_index, 1) for tile in tiles]
        upper = jnp.where(row < limit, pick(tiles[0], half_rows + 4, 0), pick(tiles[1], half_rows + 4, 0))
        return jnp.concatenate([pick(tiles[0], half_rows, 0), upper], axis=0)

    lifted = [finer(Q2[H2 + x], 3, half_lanes) for x in range(-3, 5)]
    for x in range(14):
        P1_16 = G1[5, x] + lifted[(x - 5) // 2 + 3]
        U1[0, x] = P1_16
    g1 = face(G1, 2), face(G1, 3), face(G1, 4)
    even_v, odd_v = U1.at[0], U1.at[1]
    weight1 = G1.at[1]
    sweep(even_v, odd_v, g1, face(G1, 0), weight1, 1, 13)
    sweep(odd_v, even_v, g1, face(G1, 0), weight1, 2, 12)
    sweep(even_v, odd_v, g1, face(G1, 0), weight1, 3, 11)

    lifted = [finer(odd_v[5 + x], 4) for x in range(-2, 6)]
    for x in range(X0):
        for part in (E, O):
            VA[x, :, part] = VP[x, :, part] + lifted[(x - 3) // 2 + 2]
    sweep0(VA, VB, 1, X0 - 1)
    sweep0(VB, VA, 2, X0 - 2)
    is_even = lax.rem(lane, 2) == 0
    for x in range(8):
        halves = []
        for v, total, part in couplings0(VA, H0 + x):
            result = 0.2 * v[0:8] + W0[H0 + x, own, part] * (F0[0, H0 + x, own, part] + total[0:8])
            halves.append(result)
        for part, index in ((E, half_lanes), (O, half_lanes + 64)):
            out[x, :, part] = jnp.where(is_even, pick(halves[0], index, 1), pick(halves[1], index, 1))

    near3y.sent(dummy)
    near2x.sent(dummy)


def solution(mesh):
    nx, ny = mesh.shape["bx"], mesh.shape["by"]

    def vmem(*shape):
        return pltpu.VMEM(shape, F32)

    def body(*args):
        return pl.pallas_call(
            functools.partial(kernel, nx, ny),
            out_shape=jax.ShapeDtypeStruct((8, 8, 256), F32),
            in_specs=[pl.BlockSpec(memory_space=pltpu.HBM)] * 5,
            out_specs=pl.BlockSpec(memory_space=pltpu.VMEM),
            scratch_shapes=[
                vmem(5, 8, 8, 256), pltpu.SemaphoreType.DMA((5,)),
                vmem(5, X0 + 1, 16, 256), vmem(8, 8, 256), vmem(8, 8, 256), vmem(8, 256), vmem(8, 8, 256),
                vmem(8, 8, 256), vmem(X0, 16, 256), vmem(X0, 16, 256), vmem(X0, 16, 256), vmem(X0, 16, 256),
                vmem(5, X1 + 1, 24, 128), vmem(X1, 24, 128), vmem(X1, 24, 128), vmem(X1, 24, 128),
                vmem(6, 14, 16, 128), vmem(2, 14, 16, 128),
                vmem(6, X2, 16, 128), vmem(2, X2, 16, 128), vmem(X2, 16, 128), vmem(X2, 16, 128), vmem(8, 16, 128), vmem(X2, 16, 128), vmem(X2, 16, 128),
                vmem(SLOTS, 1, 128), vmem(4, SLOTS, 1, 128), vmem(GROUPS, 8, 128), vmem(4, GROUPS, 8, 128),
                vmem(5, GROUPS, 16, 128), vmem(GROUPS, 16, 128), vmem(GROUPS, 16, 128), vmem(GROUPS, 16, 128),
                vmem(8192, 128),
                pltpu.SemaphoreType.DMA((16,)), pltpu.SemaphoreType.DMA((16,)),
            ],
            compiler_params=pltpu.CompilerParams(
                collective_id=0, has_side_effects=True, vmem_limit_bytes=64 * 2**20
            ),
        )(*args)

    return jax.shard_map(
        body,
        mesh=mesh,
        in_specs=(P("bx", "by", None),) * 5,
        out_specs=P("bx", "by", None),
        check_vma=False,
    )
```

```python
import functools

import jax
import jax.numpy as jnp
from jax import lax
from jax.experimental import pallas as pl
from jax.experimental.pallas import tpu as pltpu
from jax.sharding import PartitionSpec as P

MESH = pl.DeviceIdType.MESH
F32 = jnp.float32
COARSE = 8

H0, H1, H2, H3 = 3, 9, 6, 10
X0, X1, X2 = 8 + 2 * H0, 4 + 2 * H1, 2 + 2 * H2
SLOTS, GROUPS = 2 * H3 + 1, (2 * H3 + 4) // 4


def reach(offset, size, halo):
    if offset == 0:
        return 0, size
    near = size * (abs(offset) - 1)
    count = min(size, halo - near)
    if count <= 0:
        return 0, 0
    return (0, count) if offset > 0 else (size - count, count)


def gap(offset, size):
    return 0 if offset == 0 else size * (abs(offset) - 1) + 1


def distance(offset):
    dx, dy = abs(offset[0]), offset[1] % 16
    return dx / 2 + min(dy % 4, 4 - dy % 4) + min(dy / 4, 4 - dy / 4)


def farthest_first(offsets):
    return sorted(offsets, key=distance, reverse=True)


AROUND = farthest_first([(a, b) for a in (-1, 0, 1) for b in (-1, 0, 1) if (a, b) != (0, 0)])
WIDE = farthest_first(
    [
        (a, b)
        for a in range(-3, 4)
        for b in range(-3, 4)
        if (a, b) != (0, 0) and gap(a, 4) + gap(b, 4) <= H1
    ]
)
ALONG_X = [dx for dx, _ in farthest_first([(a, 0) for a in range(-H3, H3 + 1) if a])]
ALONG_Y = [dy for _, dy in farthest_first([(0, b) for b in range(1, 16)])]
NEAR = [-2, 2, -3, 3, -1, 1]
PARTNERS = farthest_first(
    sorted(set(WIDE) | {(a, 0) for a in ALONG_X} | {(0, b if b <= 8 else b - 16) for b in ALONG_Y})
)


def lanes(shape=(8, 128)):
    return lax.broadcasted_iota(jnp.int32, shape, 1)


def rows(shape=(8, 128)):
    return lax.broadcasted_iota(jnp.int32, shape, 0)


def pick(tile, index, axis):
    return jnp.take_along_axis(tile, index, axis=axis, mode="promise_in_bounds")


def up(value):
    return pltpu.roll(value, value.shape[0] - 1, 0)


def down(value):
    return pltpu.roll(value, 1, 0)


def right(value):
    return pltpu.roll(value, 127, 1)


def left(value):
    return pltpu.roll(value, 1, 1)


def coarsen(planes, kind, lane_index=None):
    out = []
    for i in range(0, len(planes), 2):
        total = planes[i] if kind == "x" else planes[i] + planes[i + 1]
        if kind != "y":
            total = total + up(total)
        total = pick(total, lax.rem(2 * rows(), 8), 0)
        if lane_index is not None:
            if kind != "z":
                total = total + right(total)
            total = pick(total, lane_index, 1)
        out.append(total * (0.125 if kind == "c" else 0.0625))
    return out


def couplings(get, bx, by, bz, x):
    v = get(x)
    cy, cz = by(x), bz(x)
    total = bx(x) * get(x - 1) + bx(x + 1) * get(x + 1)
    total = total + cy * down(v) + up(cy * v)
    return v, total + cz * left(v) + right(cz * v)


class Copies:
    def __init__(self, place, send_sems, recv_sems, number):
        self.place, self.number = place, number
        self.send_sem, self.recv_sem = send_sems.at[number], recv_sems.at[number]
        self.count = 0

    def start(self, source, target, offset):
        pltpu.make_async_remote_copy(
            src_ref=source,
            dst_ref=target,
            send_sem=self.send_sem,
            recv_sem=self.recv_sem,
            device_id=self.place(offset),
            device_id_type=MESH,
        ).start()
        size = 1
        for dim in source.shape:
            size *= dim
        self.count += size // 128

    def _wait(self, sem, dummy):
        part = dummy.at[pl.ds(0, self.count)]
        pltpu.make_async_copy(part, part, sem).wait()

    def arrived(self, dummy):
        self._wait(self.recv_sem, dummy)

    def sent(self, dummy):
        self._wait(self.send_sem, dummy)


def kernel(nx, ny, rhs, acoef, beta_x, beta_y, beta_z, out,
           IN, in_sems, F0, A0, E0, HX, HY, D0, G0, W0, VA, VB, VP,
           F1, W1, P1, Q1, G1, U1,
           F2, S2, T2, W2, FP, P2, Q2,
           R3, RC, PK, PC, F3, W3, P3, Q3,
           dummy, send_sems, recv_sems):
    ix, iy = lax.axis_index("bx"), lax.axis_index("by")
    loads = [
        pltpu.make_async_copy(ref, IN.at[number], in_sems.at[number])
        for number, ref in enumerate((beta_x, beta_y, beta_z, acoef, rhs))
    ]
    for load in loads:
        load.start()

    def place(offset):
        return (lax.rem(ix + (offset[0] % nx), nx), lax.rem(iy + (offset[1] % ny), ny))

    def group(number):
        return Copies(place, send_sems, recv_sems, number)

    barrier = pltpu.get_barrier_semaphore()
    for offset in PARTNERS:
        pl.semaphore_signal(barrier, inc=1, device_id=place(offset), device_id_type=MESH)

    lane, row = lanes(), rows()
    even = lax.rem(2 * lane, 128)
    keep_x = jnp.where(ix == 0, 0.0, 1.0).astype(F32)
    keep_y = jnp.where(iy == 0, 0.0, 1.0).astype(F32)
    keep_rows = jnp.where(row == 0, keep_y, 1.0)
    E, O = pl.ds(0, 128), pl.ds(128, 128)

    def split(number, x):
        low, high = IN[number, x, :, E], IN[number, x, :, O]
        return tuple(
            jnp.where(lane < 64, pick(low, even + odd, 1), pick(high, even + odd, 1)) for odd in (0, 1)
        )

    own = pl.ds(0, 8)
    for load in loads:
        load.wait()
    for x in range(8):
        px = H0 + x
        bx, by, bz, a, f = (split(number, x) for number in range(5))
        for half, part in ((0, E), (1, O)):
            bxm = bx[half] * keep_x if x == 0 else bx[half]
            bym = by[half] * keep_rows
            extra = by[half] - bym
            if x == 0:
                extra = extra + (bx[half] - bxm)
            bzm = bz[half]
            if half == 0:
                bzm = jnp.where(lane == 0, 0.0, bzm)
                extra = extra + (bz[half] - bzm)
            F0[0, px, own, part] = f[half]
            F0[1, px, own, part] = a[half] + extra
            F0[2, px, own, part] = bxm
            F0[3, px, own, part] = bym
            F0[4, px, own, part] = bzm
            A0[x, :, part] = a[half]
            E0[x, :, part] = extra

    for x in range(8):
        for half, part in ((0, E), (1, O)):
            bx, by, bz = (F0[n, H0 + x, own, part] for n in (2, 3, 4))
            total = F0[1, H0 + x, own, part] + bx + by + up(by) + bz
            if x < 7:
                total = total + F0[2, H0 + x + 1, own, part]
            D0[x, :, part] = total + (F0[4, H0 + x, own, O] if half == 0 else right(F0[4, H0 + x, own, E]))

    def both(get):
        return [get(x, E) + get(x, O) for x in range(8)]

    to64, to32 = even, lax.rem(2 * lane, 64)
    a1 = coarsen(both(lambda x, p: A0[x, :, p]), "c")
    e1 = [0.5 * t for t in coarsen(both(lambda x, p: E0[x, :, p]), "c")]
    bx1 = coarsen(both(lambda x, p: F0[2, H0 + x, own, p]), "x")
    by1 = coarsen(both(lambda x, p: F0[3, H0 + x, own, p]), "y")
    bz1 = coarsen([F0[4, H0 + x, own, E] for x in range(8)], "z")
    a2 = coarsen(a1, "c", to64)
    e2 = [0.5 * t for t in coarsen(e1, "c", to64)]
    bx2, by2, bz2 = coarsen(bx1, "x", to64), coarsen(by1, "y", to64), coarsen(bz1, "z", to64)
    a3 = coarsen(a2, "c", to32)
    e3 = [0.5 * t for t in coarsen(e2, "c", to32)]
    bx3, by3, bz3 = coarsen(bx2, "x", to32), coarsen(by2, "y", to32), coarsen(bz2, "z", to32)

    for number, field in enumerate((bx1, by1, bz1)):
        for i in range(4):
            F1[2 + number, H1 + i, pl.ds(0, 4)] = field[i][0:4]

    def wide_spans(dx, dy):
        fx, cx = reach(-dx, 4, H1)
        fy, cy = reach(-dy, 4, H1)
        return pl.ds(H1 + fx, cx), pl.ds(fy, cy), pl.ds(H1 - 4 * dx + fx, cx), pl.ds((fy - 4 * dy) % 24, cy)

    def send1(numbers, offset, collection):
        sx, sy, tx, ty = wide_spans(*offset)
        collection.start(F1.at[numbers, sx, sy], F1.at[numbers, tx, ty], offset)

    pl.semaphore_wait(barrier, len(PARTNERS))

    faces = group(0)
    faces.start(F0.at[2, H0, own], HX.at[:, :], (-1, 0))
    faces.start(F0.at[3, pl.ds(H0, 8), pl.ds(0, 1)], HY.at[:, pl.ds(0, 1)], (0, -1))
    halo = group(1)

    def span_x(offset, wide):
        if offset == 0:
            return pl.ds(H0, 8), pl.ds(H0, 8)
        if offset < 0:
            return pl.ds(H0, wide), pl.ds(H0 + 8, wide)
        return pl.ds(H0 + 8 - wide, wide), pl.ds(H0 - wide, wide)

    def span_y(offset, wide):
        if offset == 0:
            return pl.ds(0, 8), pl.ds(0, 8)
        if offset < 0:
            return pl.ds(0, wide), pl.ds(8, wide)
        return pl.ds(8 - wide, wide), pl.ds(16 - wide, wide)

    def spans(dx, dy):
        width = 2 if dx != 0 and dy != 0 else 3
        sx, tx = span_x(dx, width)
        sy, ty = span_y(dy, width)
        return sx, sy, tx, ty

    for dx, dy, number, x, y in (
        (-1, -1, 2, 2, 0), (-1, -1, 3, 2, 0), (-1, -1, 2, 0, 2), (-1, -1, 3, 0, 2),
        (-1, 1, 2, 2, 7), (-1, 1, 2, 0, 5), (1, -1, 3, 7, 2), (1, -1, 3, 5, 0),
    ):
        source = F0.at[number, H0 + x, pl.ds(y, 1)]
        halo.start(source, F0.at[number, H0 + x - 8 * dx, pl.ds((y - 8 * dy) % 16, 1)], (dx, dy))
    for dx, dy in AROUND:
        if dx and dy:
            sx, sy, tx, ty = spans(dx, dy)
            halo.start(F0.at[:, sx, sy], F0.at[:, tx, ty], (dx, dy))
    planes = pl.ds(H0, 8)
    for dy in (-1, 1):
        near, far, there, beyond = (0, 2, 8, 10) if dy < 0 else (6, 5, 14, 13)
        halo.start(F0.at[:, planes, pl.ds(near, 2)], F0.at[:, planes, pl.ds(there, 2)], (0, dy))
        halo.start(F0.at[0, planes, pl.ds(far, 1)], F0.at[0, planes, pl.ds(beyond, 1)], (0, dy))
        halo.start(D0.at[:, pl.ds(far, 1)], F0.at[1, planes, pl.ds(beyond, 1)], (0, dy))
        if dy < 0:
            halo.start(F0.at[3, planes, pl.ds(far, 1)], F0.at[3, planes, pl.ds(beyond, 1)], (0, dy))
    for dx in (-1, 1):
        sx, sy, tx, ty = spans(dx, 0)
        halo.start(F0.at[:, sx, sy], F0.at[:, tx, ty], (dx, 0))
    halo.start(F0.at[2, H0 + 3, own], F0.at[2, H0 + 11, own], (-1, 0))

    faces1y = group(2)
    for dy in NEAR:
        send1(pl.ds(2, 3), (0, dy), faces1y)

    faces.arrived(dummy)
    hx = HX[:, E] + HX[:, O]
    hx1 = coarsen([hx, hx], "x")[0]
    hx2 = coarsen([hx1, hx1], "x", to64)[0]
    hx3 = coarsen([hx2, hx2], "x", to32)[0]
    hy = [HY[x, :, E] + HY[x, :, O] for x in range(8)]
    hy1 = [0.0625 * (hy[2 * i] + hy[2 * i + 1]) for i in range(4)]

    def squeeze(t, index):
        return pick(t + right(t), index, 1) * 0.0625

    hy2 = [squeeze(hy1[2 * i] + hy1[2 * i + 1], to64) for i in range(2)]
    hy3 = squeeze(hy2[0] + hy2[1], to32)

    def diag_of(a, e, bx, by, bz, hx_plane, hy_rows, last):
        result = []
        for i in range(len(a)):
            high_x = bx[i + 1] if i + 1 < len(a) else hx_plane
            edge = pltpu.roll(hy_rows[i], last, 0) if last else hy_rows[i]
            high_y = jnp.where(row == last, edge, up(by[i]))
            result.append(a[i] + e[i] + bx[i] + high_x + by[i] + high_y + bz[i] + right(bz[i]))
        return result

    d1 = diag_of(a1, e1, bx1, by1, bz1, hx1, hy1, 3)
    d2 = diag_of(a2, e2, bx2, by2, bz2, hx2, hy2, 1)
    d3 = diag_of(a3, e3, bx3, by3, bz3, hx3, [hy3], 0)
    for i in range(4):
        F1[1, H1 + i, pl.ds(0, 4)] = d1[i][0:4]
    two = pl.ds(0, 2)
    mid = pl.ds(H2, 2)
    for i in range(2):
        own2 = [jnp.where(lane < 64, a, b) for a, b in ((d2[i], bx2[i]), (by2[i], bz2[i]))]
        for number in range(2):
            S2[number, H2 + i, two] = own2[number][0:2]
    for number, field in enumerate((d3, bx3, by3, bz3)):
        RC[number, H3] = field[0][0:1]

    diag1y = group(3)
    for dy in NEAR:
        send1(pl.ds(1, 1), (0, dy), diag1y)
    coef1x = group(4)
    for dx in NEAR:
        send1(pl.ds(1, 4), (dx, 0), coef1x)
    coef2y = group(6)
    for dy in NEAR:
        coef2y.start(S2.at[:, mid, two], S2.at[:, mid, pl.ds((-2 * dy) % 16, 2)], (0, dy))
    coef3x = group(8)
    for dx in ALONG_X:
        coef3x.start(RC.at[:, H3], RC.at[:, H3 - dx], (dx, 0))

    halo.arrived(dummy)
    for x in range(X0):
        hz = F0[4, x, :, E], F0[4, x, :, O]
        for half, part in ((0, E), (1, O)):
            by = F0[3, x, :, part]
            total = F0[1, x, :, part] + F0[2, x, :, part] + F0[2, x + 1, :, part] + by + up(by) + hz[half]
            total = total + (hz[1] if half == 0 else right(hz[0]))
            if H0 <= x < H0 + 8:
                known = F0[1, x, pl.ds(8, 8), part]
                if x == H0 + 7:
                    known = known + F0[2, x + 1, pl.ds(8, 8), part]
                outer = jnp.where((row == 2) | (row == 5), known, total[8:16])
                total = jnp.concatenate([total[0:8], outer], axis=0)
            w = 0.8 / total
            W0[x, :, part] = w
            VA[x, :, part] = w * F0[0, x, :, part]
            if H0 <= x < H0 + 8:
                G0[x - H0, :, part] = total[0:8]

    def couplings0(src, x, count=16):
        ve, vo = src[x, :, E], src[x, :, O]
        ze, zo = F0[4, x, :, E], F0[4, x, :, O]
        sums = []
        for v, part in ((ve, E), (vo, O)):
            by = F0[3, x, :, part]
            total = F0[2, x, :, part] * src[x - 1, :, part] + F0[2, x + 1, :, part] * src[x + 1, :, part]
            sums.append(total + by * down(v) + up(by * v))
        sums[0] = sums[0] + ze * left(vo) + zo * vo
        sums[1] = sums[1] + zo * ve + right(ze * ve)
        return ((ve, sums[0], E), (vo, sums[1], O))

    def sweep0(src, dst, first, last):
        for x in range(first, last):
            for v, total, part in couplings0(src, x):
                dst[x, :, part] = 0.2 * v + W0[x, :, part] * (F0[0, x, :, part] + total)

    sweep0(VA, VB, 1, X0 - 1)
    sweep0(VB, VA, 2, X0 - 2)
    remains = []
    for x in range(8):
        parts = []
        for v, total, part in couplings0(VA, H0 + x):
            v, total = v[0:8], total[0:8]
            parts.append(F0[0, H0 + x, own, part] + total - G0[x, :, part] * v)
            VP[H0 + x, own, part] = v
        remains.append(parts[0] + parts[1])
    f1 = coarsen(remains, "c")
    for i in range(4):
        F1[0, H1 + i, pl.ds(0, 4)] = f1[i][0:4]

    wide_f = group(9)
    for offset in WIDE:
        sx, sy, tx, ty = wide_spans(*offset)
        wide_f.start(F1.at[0, sx, sy], F1.at[0, tx, ty], offset)

    faces1y.arrived(dummy)
    diag1y.arrived(dummy)
    corner1x = group(5)
    for dx in (-2, -1, 1, 2):
        fx, cx = reach(-dx, 4, H1)
        for first, count in ((4, 4), (20, 4)) if abs(dx) == 2 else ((4, 4), (8, 4), (16, 8)):
            span = pl.ds(first, count)
            corner1x.start(
                F1.at[pl.ds(1, 4), pl.ds(H1 + fx, cx), span],
                F1.at[pl.ds(1, 4), pl.ds(H1 - 4 * dx + fx, cx), span],
                (dx, 0),
            )

    def along_x2(collection, ref, lead):
        for dx in NEAR:
            for first, count in {1: ((0, 8), (10, 6)), 2: ((0, 5), (13, 3)), 3: ((0, 3), (15, 1))}[abs(dx)]:
                source = ref.at[(*lead, mid, pl.ds(first, count))]
                collection.start(source, ref.at[(*lead, pl.ds(H2 - 2 * dx, 2), pl.ds(first, count))], (dx, 0))

    coef2y.arrived(dummy)
    coef2x = group(7)
    along_x2(coef2x, S2, (slice(None),))

    def packed(get):
        result = []
        for g in range(GROUPS):
            columns = [get(min(4 * g + k, SLOTS - 1)) for k in range(4)]
            line = lane[0:1]
            result.append(
                jnp.where(
                    line < 64,
                    jnp.where(line < 32, columns[0], columns[1]),
                    jnp.where(line < 96, columns[2], columns[3]),
                )
            )
        return result

    one = pl.ds(0, 1)
    coef3x.arrived(dummy)
    for number in range(4):
        for g, value in enumerate(packed(lambda s: RC[number, s])):
            PC[number, g, one] = value
            F3[1 + number, g, one] = value
    coef1x.arrived(dummy)
    corner1x.arrived(dummy)
    for x in range(X1):
        W1[x] = 0.8 / F1[1, x]
    coef2x.arrived(dummy)
    wide_lanes = lanes((16, 128))

    def unpacked(value):
        swapped = pltpu.roll(value, 64, 1)
        return jnp.where(wide_lanes < 64, value, swapped), jnp.where(wide_lanes < 64, swapped, value)

    for x in range(X2):
        F2[2, x], F2[3, x] = unpacked(S2[0, x])
        F2[4, x], F2[5, x] = unpacked(S2[1, x])
        W2[x] = 0.8 / F2[2, x]

    def face(ref, number):
        return lambda x: ref[number, x]

    def sweep(src, dst, coeffs, source, weight, first, last, shift=0):
        for x in range(first, last):
            v, total = couplings(lambda p: src[p - shift], *coeffs, x)
            dst[x - shift] = 0.2 * v + weight[x] * (source(x) + total)

    c1 = face(F1, 2), face(F1, 3), face(F1, 4)
    wide_f.arrived(dummy)
    for x in range(X1):
        P1[x] = W1[x] * F1[0, x]
    sweep(P1, Q1, c1, face(F1, 0), W1, 1, X1 - 1)
    sweep(Q1, P1, c1, face(F1, 0), W1, 2, X1 - 2)

    def remains1(x):
        v, total = couplings(lambda p: P1[p], *c1, x)
        return F1[0, x] + total - F1[1, x] * v

    pairs = lax.rem(2 * row, 8)
    for i in range(8):
        x = H1 - 6 + 2 * i
        total = remains1(x) + remains1(x + 1)
        tiles = []
        for t in range(3):
            tile = total[8 * t : 8 * t + 8]
            tiles.append(pick(tile + up(tile), pairs, 0))
        tiles = [jnp.where(row < 4, tiles[0], tiles[1]), tiles[2]]
        tiles = [pick(tile + right(tile), to64, 1) * 0.125 for tile in tiles]
        FP[i] = jnp.concatenate(tiles, axis=0)

    c2 = face(F2, 3), face(F2, 4), face(F2, 5)
    for i in range(8):
        P2[i] = W2[i + 3] * FP[i]
    sweep(P2, Q2, c2, lambda x: FP[x - 3], W2, 4, 10, 3)
    sweep(Q2, P2, c2, lambda x: FP[x - 3], W2, 5, 9, 3)
    total = None
    for x in (6, 7):
        v, s = couplings(lambda p: P2[p - 3], *c2, x)
        rest = (FP[x - 3] + s - F2[2, x] * v)[0:8]
        total = rest if total is None else total + rest
        T2[x, two] = jnp.where(lane < 64, FP[x - 3][0:8], v[0:8])[0:2]
    total = total + up(total)
    f3 = (pick(total + right(total), to32, 1) * 0.125)[0:1]
    R3[H3] = f3

    near3x = group(10)
    for dx in ALONG_X:
        near3x.start(R3.at[H3], R3.at[H3 - dx], (dx, 0))
    near2y = group(11)
    for dy in NEAR:
        near2y.start(T2.at[mid, two], T2.at[mid, pl.ds((-2 * dy) % 16, 2)], (0, dy))
    coef3y = group(13)
    for dy in ALONG_Y:
        coef3y.start(PC.at[:, :, one], F3.at[pl.ds(1, 4), :, pl.ds(16 - dy, 1)], (0, dy))
    halo_v = group(12)
    for dx, dy in AROUND:
        sx, sy, tx, ty = spans(dx, dy)
        halo_v.start(VP.at[sx, sy], VP.at[tx, ty], (dx, dy))

    for x in range(14):
        p = H1 - 5 + x
        for number, get in enumerate((face(F1, 0), lambda q: W1[q], face(F1, 2), face(F1, 3), face(F1, 4), lambda q: P1[q])):
            value = get(p)
            mixed = jnp.where(row < 3, value[8:16], value[16:24])
            G1[number, x] = jnp.concatenate([value[0:8], mixed], axis=0)
    near3x.arrived(dummy)
    for g, value in enumerate(packed(lambda s: R3[s])):
        PK[g, one] = value
        F3[0, g, one] = value
    near3y = group(14)
    for dy in ALONG_Y:
        near3y.start(PK.at[:, one], F3.at[0, :, pl.ds(16 - dy, 1)], (0, dy))
    near2y.arrived(dummy)
    near2x = group(15)
    along_x2(near2x, T2, ())
    coef3y.arrived(dummy)
    for g in range(GROUPS):
        W3[g] = 0.8 / F3[1, g]
    halo_v.arrived(dummy)
    for done in (faces, halo, faces1y, diag1y, coef1x, coef2y, coef3x, wide_f, corner1x, coef2x, near3x, near2y, coef3y, halo_v):
        done.sent(dummy)

    near3y.arrived(dummy)
    line = lanes((16, 128))
    for g in range(GROUPS):
        P3[g] = W3[g] * F3[0, g]
    src, dst = P3, Q3
    for step in range(COARSE - 1):
        for g in range(GROUPS):
            v, cx, cy, cz = src[g], F3[2, g], F3[3, g], F3[4, g]
            ahead = min(g + 1, GROUPS - 1)
            low = jnp.where(line < 32, pltpu.roll(src[max(g - 1, 0)], 32, 1), pltpu.roll(v, 32, 1))
            high = jnp.where(
                line >= 96, pltpu.roll(F3[2, ahead] * src[ahead], 96, 1), pltpu.roll(cx * v, 96, 1)
            )
            total = cx * low + high + cy * down(v) + up(cy * v) + cz * left(v) + right(cz * v)
            dst[g] = 0.2 * v + W3[g] * (F3[0, g] + total)
        src, dst = dst, src

    half_rows = lax.shift_right_logical(row, 1)

    def onto2(x):
        slot = H3 + x
        index = 32 * (slot % 4) + lax.shift_right_logical(lax.rem(lane, 64), 1)
        value = src[slot // 4]
        low, high = (pick(value[8 * t : 8 * t + 8], index, 1) for t in (0, 1))
        return jnp.concatenate([pick(low, half_rows, 0), pick(high, half_rows + 4, 0)], axis=0)

    lifted = [onto2(x) for x in range(-3, 4)]
    near2x.arrived(dummy)
    for x in range(X2):
        F2[0, x], value = unpacked(T2[x])
        P2[x] = value + lifted[x // 2]
    sweep(P2, Q2, c2, face(F2, 0), W2, 1, X2 - 1)
    sweep(Q2, P2, c2, face(F2, 0), W2, 2, X2 - 2)
    sweep(P2, Q2, c2, face(F2, 0), W2, 3, X2 - 3)

    half_lanes = lax.shift_right_logical(lane, 1)

    def finer(value, limit, lane_index=None):
        tiles = [value[0:8], value[8:16]]
        if lane_index is not None:
            tiles = [pick(tile, lane_index, 1) for tile in tiles]
        upper = jnp.where(row < limit, pick(tiles[0], half_rows + 4, 0), pick(tiles[1], half_rows + 4, 0))
        return jnp.concatenate([pick(tiles[0], half_rows, 0), upper], axis=0)

    lifted = [finer(Q2[H2 + x], 3, half_lanes) for x in range(-3, 5)]
    for x in range(14):
        P1_16 = G1[5, x] + lifted[(x - 5) // 2 + 3]
        U1[0, x] = P1_16
    g1 = face(G1, 2), face(G1, 3), face(G1, 4)
    even_v, odd_v = U1.at[0], U1.at[1]
    weight1 = G1.at[1]
    sweep(even_v, odd_v, g1, face(G1, 0), weight1, 1, 13)
    sweep(odd_v, even_v, g1, face(G1, 0), weight1, 2, 12)
    sweep(even_v, odd_v, g1, face(G1, 0), weight1, 3, 11)

    lifted = [finer(odd_v[5 + x], 4) for x in range(-2, 6)]
    for x in range(X0):
        for part in (E, O):
            VA[x, :, part] = VP[x, :, part] + lifted[(x - 3) // 2 + 2]
    sweep0(VA, VB, 1, X0 - 1)
    sweep0(VB, VA, 2, X0 - 2)
    is_even = lax.rem(lane, 2) == 0
    for x in range(8):
        halves = []
        for v, total, part in couplings0(VA, H0 + x):
            result = 0.2 * v[0:8] + W0[H0 + x, own, part] * (F0[0, H0 + x, own, part] + total[0:8])
            halves.append(result)
        for part, index in ((E, half_lanes), (O, half_lanes + 64)):
            out[x, :, part] = jnp.where(is_even, pick(halves[0], index, 1), pick(halves[1], index, 1))

    near3y.sent(dummy)
    near2x.sent(dummy)


def solution(mesh):
    nx, ny = mesh.shape["bx"], mesh.shape["by"]

    def vmem(*shape):
        return pltpu.VMEM(shape, F32)

    def body(*args):
        return pl.pallas_call(
            functools.partial(kernel, nx, ny),
            out_shape=pltpu.VMEM((8, 8, 256), F32),
            in_specs=[pl.BlockSpec(memory_space=pltpu.HBM)] * 5,
            out_specs=pl.BlockSpec(memory_space=pltpu.VMEM),
            scratch_shapes=[
                vmem(5, 8, 8, 256), pltpu.SemaphoreType.DMA((5,)),
                vmem(5, X0 + 1, 16, 256), vmem(8, 8, 256), vmem(8, 8, 256), vmem(8, 256), vmem(8, 8, 256),
                vmem(8, 8, 256), vmem(8, 8, 256), vmem(X0, 16, 256), vmem(X0, 16, 256), vmem(X0, 16, 256), vmem(X0, 16, 256),
                vmem(5, X1 + 1, 24, 128), vmem(X1, 24, 128), vmem(X1, 24, 128), vmem(X1, 24, 128),
                vmem(6, 14, 16, 128), vmem(2, 14, 16, 128),
                vmem(6, X2, 16, 128), vmem(2, X2, 16, 128), vmem(X2, 16, 128), vmem(X2, 16, 128), vmem(8, 16, 128), vmem(X2, 16, 128), vmem(X2, 16, 128),
                vmem(SLOTS, 1, 128), vmem(4, SLOTS, 1, 128), vmem(GROUPS, 8, 128), vmem(4, GROUPS, 8, 128),
                vmem(5, GROUPS, 16, 128), vmem(GROUPS, 16, 128), vmem(GROUPS, 16, 128), vmem(GROUPS, 16, 128),
                vmem(8192, 128),
                pltpu.SemaphoreType.DMA((16,)), pltpu.SemaphoreType.DMA((16,)),
            ],
            compiler_params=pltpu.CompilerParams(
                collective_id=0, has_side_effects=True, vmem_limit_bytes=60 * 2**20
            ),
        )(*args)

    return jax.shard_map(
        body,
        mesh=mesh,
        in_specs=(P("bx", "by", None),) * 5,
        out_specs=P("bx", "by", None),
        check_vma=False,
    )
```

```python
import functools

import jax
import jax.numpy as jnp
from jax import lax
from jax.experimental import pallas as pl
from jax.experimental.pallas import tpu as pltpu
from jax.sharding import PartitionSpec as P

MESH = pl.DeviceIdType.MESH
F32 = jnp.float32
COARSE = 8

H0, H1, H2, H3 = 3, 9, 6, 10
X0, X1, X2 = 8 + 2 * H0, 4 + 2 * H1, 2 + 2 * H2
SLOTS, GROUPS = 2 * H3 + 1, (2 * H3 + 4) // 4


def reach(offset, size, halo):
    if offset == 0:
        return 0, size
    near = size * (abs(offset) - 1)
    count = min(size, halo - near)
    if count <= 0:
        return 0, 0
    return (0, count) if offset > 0 else (size - count, count)


def gap(offset, size):
    return 0 if offset == 0 else size * (abs(offset) - 1) + 1


def distance(offset):
    dx, dy = abs(offset[0]), offset[1] % 16
    return dx / 2 + min(dy % 4, 4 - dy % 4) + min(dy / 4, 4 - dy / 4)


def farthest_first(offsets):
    return sorted(offsets, key=distance, reverse=True)


AROUND = farthest_first([(a, b) for a in (-1, 0, 1) for b in (-1, 0, 1) if (a, b) != (0, 0)])
WIDE = farthest_first(
    [
        (a, b)
        for a in range(-3, 4)
        for b in range(-3, 4)
        if (a, b) != (0, 0) and gap(a, 4) + gap(b, 4) <= H1
    ]
)
ALONG_X = [dx for dx, _ in farthest_first([(a, 0) for a in range(-H3, H3 + 1) if a])]
ALONG_Y = [dy for _, dy in farthest_first([(0, b) for b in range(1, 16)])]
NEAR = [-2, 2, -3, 3, -1, 1]
PARTNERS = farthest_first(
    sorted(set(WIDE) | {(a, 0) for a in ALONG_X} | {(0, b if b <= 8 else b - 16) for b in ALONG_Y})
)


def lanes(shape=(8, 128)):
    return lax.broadcasted_iota(jnp.int32, shape, 1)


def rows(shape=(8, 128)):
    return lax.broadcasted_iota(jnp.int32, shape, 0)


def pick(tile, index, axis):
    return jnp.take_along_axis(tile, index, axis=axis, mode="promise_in_bounds")


def up(value):
    return pltpu.roll(value, value.shape[0] - 1, 0)


def down(value):
    return pltpu.roll(value, 1, 0)


def right(value):
    return pltpu.roll(value, 127, 1)


def left(value):
    return pltpu.roll(value, 1, 1)


def coarsen(planes, kind, lane_index=None):
    out = []
    for i in range(0, len(planes), 2):
        total = planes[i] if kind == "x" else planes[i] + planes[i + 1]
        if kind != "y":
            total = total + up(total)
        total = pick(total, lax.rem(2 * rows(), 8), 0)
        if lane_index is not None:
            if kind != "z":
                total = total + right(total)
            total = pick(total, lane_index, 1)
        out.append(total * (0.125 if kind == "c" else 0.0625))
    return out


def couplings(get, bx, by, bz, x):
    v = get(x)
    cy, cz = by(x), bz(x)
    total = bx(x) * get(x - 1) + bx(x + 1) * get(x + 1)
    total = total + cy * down(v) + up(cy * v)
    return v, total + cz * left(v) + right(cz * v)


class Copies:
    def __init__(self, place, send_sems, recv_sems, number):
        self.place, self.number = place, number
        self.send_sem, self.recv_sem = send_sems.at[number], recv_sems.at[number]
        self.count = 0

    def start(self, source, target, offset):
        pltpu.make_async_remote_copy(
            src_ref=source,
            dst_ref=target,
            send_sem=self.send_sem,
            recv_sem=self.recv_sem,
            device_id=self.place(offset),
            device_id_type=MESH,
        ).start()
        size = 1
        for dim in source.shape:
            size *= dim
        self.count += size // 128

    def _wait(self, sem, dummy):
        part = dummy.at[pl.ds(0, self.count)]
        pltpu.make_async_copy(part, part, sem).wait()

    def arrived(self, dummy):
        self._wait(self.recv_sem, dummy)

    def sent(self, dummy):
        self._wait(self.send_sem, dummy)


def kernel(nx, ny, rhs, acoef, beta_x, beta_y, beta_z, out,
           IN, in_sems, F0, A0, E0, HX, HY, D0, G0, W0, VA, VB, VP,
           F1, D1, W1, P1, Q1, G1, U1,
           F2, S2, T2, W2, FP, P2, Q2,
           R3, RC, PK, PC, F3, W3, P3, Q3,
           dummy, send_sems, recv_sems):
    ix, iy = lax.axis_index("bx"), lax.axis_index("by")
    loads = [
        pltpu.make_async_copy(ref, IN.at[number], in_sems.at[number])
        for number, ref in enumerate((beta_x, beta_y, beta_z, acoef, rhs))
    ]
    for load in loads:
        load.start()

    def place(offset):
        return (lax.rem(ix + (offset[0] % nx), nx), lax.rem(iy + (offset[1] % ny), ny))

    def group(number):
        return Copies(place, send_sems, recv_sems, number)

    barrier = pltpu.get_barrier_semaphore()
    for offset in PARTNERS:
        pl.semaphore_signal(barrier, inc=1, device_id=place(offset), device_id_type=MESH)

    lane, row = lanes(), rows()
    even = lax.rem(2 * lane, 128)
    keep_x = jnp.where(ix == 0, 0.0, 1.0).astype(F32)
    keep_y = jnp.where(iy == 0, 0.0, 1.0).astype(F32)
    keep_rows = jnp.where(row == 0, keep_y, 1.0)
    E, O = pl.ds(0, 128), pl.ds(128, 128)

    def split(number, x):
        low, high = IN[number, x, :, E], IN[number, x, :, O]
        return tuple(
            jnp.where(lane < 64, pick(low, even + odd, 1), pick(high, even + odd, 1)) for odd in (0, 1)
        )

    own = pl.ds(0, 8)
    for load in loads:
        load.wait()
    for x in range(8):
        px = H0 + x
        bx, by, bz, a, f = (split(number, x) for number in range(5))
        for half, part in ((0, E), (1, O)):
            bxm = bx[half] * keep_x if x == 0 else bx[half]
            bym = by[half] * keep_rows
            extra = by[half] - bym
            if x == 0:
                extra = extra + (bx[half] - bxm)
            bzm = bz[half]
            if half == 0:
                bzm = jnp.where(lane == 0, 0.0, bzm)
                extra = extra + (bz[half] - bzm)
            F0[0, px, own, part] = f[half]
            F0[1, px, own, part] = a[half] + extra
            F0[2, px, own, part] = bxm
            F0[3, px, own, part] = bym
            F0[4, px, own, part] = bzm
            A0[x, :, part] = a[half]
            E0[x, :, part] = extra

    for x in range(8):
        for half, part in ((0, E), (1, O)):
            bx, by, bz = (F0[n, H0 + x, own, part] for n in (2, 3, 4))
            total = F0[1, H0 + x, own, part] + bx + by + up(by) + bz
            if x < 7:
                total = total + F0[2, H0 + x + 1, own, part]
            D0[x, :, part] = total + (F0[4, H0 + x, own, O] if half == 0 else right(F0[4, H0 + x, own, E]))

    def both(get):
        return [get(x, E) + get(x, O) for x in range(8)]

    to64, to32 = even, lax.rem(2 * lane, 64)
    a1 = coarsen(both(lambda x, p: A0[x, :, p]), "c")
    e1 = [0.5 * t for t in coarsen(both(lambda x, p: E0[x, :, p]), "c")]
    bx1 = coarsen(both(lambda x, p: F0[2, H0 + x, own, p]), "x")
    by1 = coarsen(both(lambda x, p: F0[3, H0 + x, own, p]), "y")
    bz1 = coarsen([F0[4, H0 + x, own, E] for x in range(8)], "z")
    a2 = coarsen(a1, "c", to64)
    e2 = [0.5 * t for t in coarsen(e1, "c", to64)]
    bx2, by2, bz2 = coarsen(bx1, "x", to64), coarsen(by1, "y", to64), coarsen(bz1, "z", to64)
    a3 = coarsen(a2, "c", to32)
    e3 = [0.5 * t for t in coarsen(e2, "c", to32)]
    bx3, by3, bz3 = coarsen(bx2, "x", to32), coarsen(by2, "y", to32), coarsen(bz2, "z", to32)

    for number, field in enumerate(([a + e for a, e in zip(a1, e1)], bx1, by1, bz1)):
        for i in range(4):
            F1[1 + number, H1 + i, pl.ds(0, 4)] = field[i][0:4]

    def wide_spans(dx, dy, more=0):
        fx, cx = reach(-dx, 4, H1 + (more if dx < 0 else 0))
        fy, cy = reach(-dy, 4, H1 + (more if dy < 0 else 0))
        return pl.ds(H1 + fx, cx), pl.ds(fy, cy), pl.ds(H1 - 4 * dx + fx, cx), pl.ds((fy - 4 * dy) % 24, cy)

    def send1(offset, collection):
        sx, sy, tx, ty = wide_spans(*offset, 1)
        collection.start(F1.at[pl.ds(1, 4), sx, sy], F1.at[pl.ds(1, 4), tx, ty], offset)

    pl.semaphore_wait(barrier, len(PARTNERS))

    faces = group(0)
    faces.start(F0.at[2, H0, own], HX.at[:, :], (-1, 0))
    faces.start(F0.at[3, pl.ds(H0, 8), pl.ds(0, 1)], HY.at[:, pl.ds(0, 1)], (0, -1))
    coef1y = group(2)
    for dy in NEAR:
        send1((0, dy), coef1y)
    halo = group(1)

    def span_x(offset, wide):
        if offset == 0:
            return pl.ds(H0, 8), pl.ds(H0, 8)
        if offset < 0:
            return pl.ds(H0, wide), pl.ds(H0 + 8, wide)
        return pl.ds(H0 + 8 - wide, wide), pl.ds(H0 - wide, wide)

    def span_y(offset, wide):
        if offset == 0:
            return pl.ds(0, 8), pl.ds(0, 8)
        if offset < 0:
            return pl.ds(0, wide), pl.ds(8, wide)
        return pl.ds(8 - wide, wide), pl.ds(16 - wide, wide)

    def spans(dx, dy):
        width = 2 if dx != 0 and dy != 0 else 3
        sx, tx = span_x(dx, width)
        sy, ty = span_y(dy, width)
        return sx, sy, tx, ty

    for dx, dy, number, x, y in (
        (-1, -1, 2, 2, 0), (-1, -1, 3, 2, 0), (-1, -1, 2, 0, 2), (-1, -1, 3, 0, 2),
        (-1, 1, 2, 2, 7), (-1, 1, 2, 0, 5), (1, -1, 3, 7, 2), (1, -1, 3, 5, 0),
    ):
        source = F0.at[number, H0 + x, pl.ds(y, 1)]
        halo.start(source, F0.at[number, H0 + x - 8 * dx, pl.ds((y - 8 * dy) % 16, 1)], (dx, dy))
    for dx, dy in AROUND:
        if dx and dy:
            sx, sy, tx, ty = spans(dx, dy)
            halo.start(F0.at[:, sx, sy], F0.at[:, tx, ty], (dx, dy))
    planes = pl.ds(H0, 8)
    for dy in (-1, 1):
        near, far, there, beyond = (0, 2, 8, 10) if dy < 0 else (6, 5, 14, 13)
        halo.start(F0.at[:, planes, pl.ds(near, 2)], F0.at[:, planes, pl.ds(there, 2)], (0, dy))
        halo.start(F0.at[0, planes, pl.ds(far, 1)], F0.at[0, planes, pl.ds(beyond, 1)], (0, dy))
        halo.start(D0.at[:, pl.ds(far, 1)], F0.at[1, planes, pl.ds(beyond, 1)], (0, dy))
        if dy < 0:
            halo.start(F0.at[3, planes, pl.ds(far, 1)], F0.at[3, planes, pl.ds(beyond, 1)], (0, dy))
    for dx in (-1, 1):
        sx, sy, tx, ty = spans(dx, 0)
        halo.start(F0.at[:, sx, sy], F0.at[:, tx, ty], (dx, 0))
    halo.start(F0.at[2, H0 + 3, own], F0.at[2, H0 + 11, own], (-1, 0))

    coef1x = group(4)
    for dx in NEAR:
        send1((dx, 0), coef1x)

    faces.arrived(dummy)
    hx = HX[:, E] + HX[:, O]
    hx1 = coarsen([hx, hx], "x")[0]
    hx2 = coarsen([hx1, hx1], "x", to64)[0]
    hx3 = coarsen([hx2, hx2], "x", to32)[0]
    hy = [HY[x, :, E] + HY[x, :, O] for x in range(8)]
    hy1 = [0.0625 * (hy[2 * i] + hy[2 * i + 1]) for i in range(4)]

    def squeeze(t, index):
        return pick(t + right(t), index, 1) * 0.0625

    hy2 = [squeeze(hy1[2 * i] + hy1[2 * i + 1], to64) for i in range(2)]
    hy3 = squeeze(hy2[0] + hy2[1], to32)

    def diag_of(a, e, bx, by, bz, hx_plane, hy_rows, last):
        result = []
        for i in range(len(a)):
            high_x = bx[i + 1] if i + 1 < len(a) else hx_plane
            edge = pltpu.roll(hy_rows[i], last, 0) if last else hy_rows[i]
            high_y = jnp.where(row == last, edge, up(by[i]))
            result.append(a[i] + e[i] + bx[i] + high_x + by[i] + high_y + bz[i] + right(bz[i]))
        return result

    d2 = diag_of(a2, e2, bx2, by2, bz2, hx2, hy2, 1)
    d3 = diag_of(a3, e3, bx3, by3, bz3, hx3, [hy3], 0)
    two = pl.ds(0, 2)
    mid = pl.ds(H2, 2)
    for i in range(2):
        own2 = [jnp.where(lane < 64, a, b) for a, b in ((d2[i], bx2[i]), (by2[i], bz2[i]))]
        for number in range(2):
            S2[number, H2 + i, two] = own2[number][0:2]
    for number, field in enumerate((d3, bx3, by3, bz3)):
        RC[number, H3] = field[0][0:1]

    coef2y = group(6)
    for dy in NEAR:
        coef2y.start(S2.at[:, mid, two], S2.at[:, mid, pl.ds((-2 * dy) % 16, 2)], (0, dy))
    coef1y.arrived(dummy)
    corner1x = group(5)
    for dx, parts in (
        (-2, ((0, 4, 4, 4), (0, 4, 19, 5), (0, 1, 8, 1))),
        (2, ((0, 4, 4, 4), (0, 4, 20, 4), (3, 1, 8, 1))),
        (-1, ((0, 4, 4, 4), (0, 4, 8, 5), (0, 4, 16, 8), (0, 1, 15, 1))),
        (1, ((0, 4, 4, 4), (0, 4, 8, 5), (0, 4, 16, 8))),
        (-3, ((0, 1, 4, 1), (0, 1, 23, 1))),
        (3, ((3, 1, 4, 1),)),
    ):
        for plane, planes_sent, first, count in parts:
            span = pl.ds(first, count)
            corner1x.start(
                F1.at[pl.ds(1, 4), pl.ds(H1 + plane, planes_sent), span],
                F1.at[pl.ds(1, 4), pl.ds(H1 + plane - 4 * dx, planes_sent), span],
                (dx, 0),
            )

    halo.arrived(dummy)
    for x in range(X0):
        hz = F0[4, x, :, E], F0[4, x, :, O]
        for half, part in ((0, E), (1, O)):
            by = F0[3, x, :, part]
            total = F0[1, x, :, part] + F0[2, x, :, part] + F0[2, x + 1, :, part] + by + up(by) + hz[half]
            total = total + (hz[1] if half == 0 else right(hz[0]))
            if H0 <= x < H0 + 8:
                known = F0[1, x, pl.ds(8, 8), part]
                if x == H0 + 7:
                    known = known + F0[2, x + 1, pl.ds(8, 8), part]
                outer = jnp.where((row == 2) | (row == 5), known, total[8:16])
                total = jnp.concatenate([total[0:8], outer], axis=0)
            w = 0.8 / total
            W0[x, :, part] = w
            VA[x, :, part] = w * F0[0, x, :, part]
            if H0 <= x < H0 + 8:
                G0[x - H0, :, part] = total[0:8]

    def couplings0(src, x, count=16):
        ve, vo = src[x, :, E], src[x, :, O]
        ze, zo = F0[4, x, :, E], F0[4, x, :, O]
        sums = []
        for v, part in ((ve, E), (vo, O)):
            by = F0[3, x, :, part]
            total = F0[2, x, :, part] * src[x - 1, :, part] + F0[2, x + 1, :, part] * src[x + 1, :, part]
            sums.append(total + by * down(v) + up(by * v))
        sums[0] = sums[0] + ze * left(vo) + zo * vo
        sums[1] = sums[1] + zo * ve + right(ze * ve)
        return ((ve, sums[0], E), (vo, sums[1], O))

    def sweep0(src, dst, first, last):
        for x in range(first, last):
            for v, total, part in couplings0(src, x):
                dst[x, :, part] = 0.2 * v + W0[x, :, part] * (F0[0, x, :, part] + total)

    sweep0(VA, VB, 1, X0 - 1)
    sweep0(VB, VA, 2, X0 - 2)
    remains = []
    for x in range(8):
        parts = []
        for v, total, part in couplings0(VA, H0 + x):
            v, total = v[0:8], total[0:8]
            parts.append(F0[0, H0 + x, own, part] + total - G0[x, :, part] * v)
            VP[H0 + x, own, part] = v
        remains.append(parts[0] + parts[1])
    f1 = coarsen(remains, "c")
    for i in range(4):
        F1[0, H1 + i, pl.ds(0, 4)] = f1[i][0:4]

    wide_f = group(9)
    for offset in WIDE:
        sx, sy, tx, ty = wide_spans(*offset)
        wide_f.start(F1.at[0, sx, sy], F1.at[0, tx, ty], offset)

    def along_x2(collection, ref, lead):
        for dx in NEAR:
            for first, count in {1: ((0, 8), (10, 6)), 2: ((0, 5), (13, 3)), 3: ((0, 3), (15, 1))}[abs(dx)]:
                source = ref.at[(*lead, mid, pl.ds(first, count))]
                collection.start(source, ref.at[(*lead, pl.ds(H2 - 2 * dx, 2), pl.ds(first, count))], (dx, 0))

    coef2y.arrived(dummy)
    coef2x = group(7)
    along_x2(coef2x, S2, (slice(None),))
    coef3x = group(8)
    for dx in ALONG_X:
        coef3x.start(RC.at[:, H3], RC.at[:, H3 - dx], (dx, 0))

    def packed(get):
        result = []
        for g in range(GROUPS):
            columns = [get(min(4 * g + k, SLOTS - 1)) for k in range(4)]
            line = lane[0:1]
            result.append(
                jnp.where(
                    line < 64,
                    jnp.where(line < 32, columns[0], columns[1]),
                    jnp.where(line < 96, columns[2], columns[3]),
                )
            )
        return result

    one = pl.ds(0, 1)
    coef1x.arrived(dummy)
    corner1x.arrived(dummy)
    for x in range(X1):
        by, bz = F1[3, x], F1[4, x]
        total = F1[1, x] + F1[2, x] + F1[2, x + 1] + by + up(by) + bz + right(bz)
        D1[x] = total
        W1[x] = 0.8 / total
    coef2x.arrived(dummy)
    wide_lanes = lanes((16, 128))

    def unpacked(value):
        swapped = pltpu.roll(value, 64, 1)
        return jnp.where(wide_lanes < 64, value, swapped), jnp.where(wide_lanes < 64, swapped, value)

    for x in range(X2):
        F2[2, x], F2[3, x] = unpacked(S2[0, x])
        F2[4, x], F2[5, x] = unpacked(S2[1, x])
        W2[x] = 0.8 / F2[2, x]

    def face(ref, number):
        return lambda x: ref[number, x]

    def sweep(src, dst, coeffs, source, weight, first, last, shift=0):
        for x in range(first, last):
            v, total = couplings(lambda p: src[p - shift], *coeffs, x)
            dst[x - shift] = 0.2 * v + weight[x] * (source(x) + total)

    c1 = face(F1, 2), face(F1, 3), face(F1, 4)
    wide_f.arrived(dummy)
    for x in range(X1):
        P1[x] = W1[x] * F1[0, x]
    sweep(P1, Q1, c1, face(F1, 0), W1, 1, X1 - 1)
    sweep(Q1, P1, c1, face(F1, 0), W1, 2, X1 - 2)

    def remains1(x):
        v, total = couplings(lambda p: P1[p], *c1, x)
        return F1[0, x] + total - D1[x] * v

    pairs = lax.rem(2 * row, 8)
    for i in range(8):
        x = H1 - 6 + 2 * i
        total = remains1(x) + remains1(x + 1)
        tiles = []
        for t in range(3):
            tile = total[8 * t : 8 * t + 8]
            tiles.append(pick(tile + up(tile), pairs, 0))
        tiles = [jnp.where(row < 4, tiles[0], tiles[1]), tiles[2]]
        tiles = [pick(tile + right(tile), to64, 1) * 0.125 for tile in tiles]
        FP[i] = jnp.concatenate(tiles, axis=0)

    c2 = face(F2, 3), face(F2, 4), face(F2, 5)
    for i in range(8):
        P2[i] = W2[i + 3] * FP[i]
    sweep(P2, Q2, c2, lambda x: FP[x - 3], W2, 4, 10, 3)
    sweep(Q2, P2, c2, lambda x: FP[x - 3], W2, 5, 9, 3)
    total = None
    for x in (6, 7):
        v, s = couplings(lambda p: P2[p - 3], *c2, x)
        rest = (FP[x - 3] + s - F2[2, x] * v)[0:8]
        total = rest if total is None else total + rest
        T2[x, two] = jnp.where(lane < 64, FP[x - 3][0:8], v[0:8])[0:2]
    total = total + up(total)
    f3 = (pick(total + right(total), to32, 1) * 0.125)[0:1]
    R3[H3] = f3

    near3x = group(10)
    for dx in ALONG_X:
        near3x.start(R3.at[H3], R3.at[H3 - dx], (dx, 0))
    near2y = group(11)
    for dy in NEAR:
        near2y.start(T2.at[mid, two], T2.at[mid, pl.ds((-2 * dy) % 16, 2)], (0, dy))
    coef3x.arrived(dummy)
    for number in range(4):
        for g, value in enumerate(packed(lambda s: RC[number, s])):
            PC[number, g, one] = value
            F3[1 + number, g, one] = value
    coef3y = group(13)
    for dy in ALONG_Y:
        coef3y.start(PC.at[:, :, one], F3.at[pl.ds(1, 4), :, pl.ds(16 - dy, 1)], (0, dy))
    halo_v = group(12)
    for dx, dy in AROUND:
        sx, sy, tx, ty = spans(dx, dy)
        halo_v.start(VP.at[sx, sy], VP.at[tx, ty], (dx, dy))

    for x in range(14):
        p = H1 - 5 + x
        for number, get in enumerate((face(F1, 0), lambda q: W1[q], face(F1, 2), face(F1, 3), face(F1, 4), lambda q: P1[q])):
            value = get(p)
            mixed = jnp.where(row < 3, value[8:16], value[16:24])
            G1[number, x] = jnp.concatenate([value[0:8], mixed], axis=0)
    near3x.arrived(dummy)
    for g, value in enumerate(packed(lambda s: R3[s])):
        PK[g, one] = value
        F3[0, g, one] = value
    near3y = group(14)
    for dy in ALONG_Y:
        near3y.start(PK.at[:, one], F3.at[0, :, pl.ds(16 - dy, 1)], (0, dy))
    near2y.arrived(dummy)
    near2x = group(15)
    along_x2(near2x, T2, ())
    coef3y.arrived(dummy)
    for g in range(GROUPS):
        W3[g] = 0.8 / F3[1, g]
    halo_v.arrived(dummy)
    for done in (faces, halo, coef1y, coef1x, coef2y, coef3x, wide_f, corner1x, coef2x, near3x, near2y, coef3y, halo_v):
        done.sent(dummy)

    near3y.arrived(dummy)
    line = lanes((16, 128))
    for g in range(GROUPS):
        P3[g] = W3[g] * F3[0, g]
    src, dst = P3, Q3
    for step in range(COARSE - 1):
        for g in range(GROUPS):
            v, cx, cy, cz = src[g], F3[2, g], F3[3, g], F3[4, g]
            ahead = min(g + 1, GROUPS - 1)
            low = jnp.where(line < 32, pltpu.roll(src[max(g - 1, 0)], 32, 1), pltpu.roll(v, 32, 1))
            high = jnp.where(
                line >= 96, pltpu.roll(F3[2, ahead] * src[ahead], 96, 1), pltpu.roll(cx * v, 96, 1)
            )
            total = cx * low + high + cy * down(v) + up(cy * v) + cz * left(v) + right(cz * v)
            dst[g] = 0.2 * v + W3[g] * (F3[0, g] + total)
        src, dst = dst, src

    half_rows = lax.shift_right_logical(row, 1)

    def onto2(x):
        slot = H3 + x
        index = 32 * (slot % 4) + lax.shift_right_logical(lax.rem(lane, 64), 1)
        value = src[slot // 4]
        low, high = (pick(value[8 * t : 8 * t + 8], index, 1) for t in (0, 1))
        return jnp.concatenate([pick(low, half_rows, 0), pick(high, half_rows + 4, 0)], axis=0)

    lifted = [onto2(x) for x in range(-3, 4)]
    near2x.arrived(dummy)
    for x in range(X2):
        F2[0, x], value = unpacked(T2[x])
        P2[x] = value + lifted[x // 2]
    sweep(P2, Q2, c2, face(F2, 0), W2, 1, X2 - 1)
    sweep(Q2, P2, c2, face(F2, 0), W2, 2, X2 - 2)
    sweep(P2, Q2, c2, face(F2, 0), W2, 3, X2 - 3)

    half_lanes = lax.shift_right_logical(lane, 1)

    def finer(value, limit, lane_index=None):
        tiles = [value[0:8], value[8:16]]
        if lane_index is not None:
            tiles = [pick(tile, lane_index, 1) for tile in tiles]
        upper = jnp.where(row < limit, pick(tiles[0], half_rows + 4, 0), pick(tiles[1], half_rows + 4, 0))
        return jnp.concatenate([pick(tiles[0], half_rows, 0), upper], axis=0)

    lifted = [finer(Q2[H2 + x], 3, half_lanes) for x in range(-3, 5)]
    for x in range(14):
        P1_16 = G1[5, x] + lifted[(x - 5) // 2 + 3]
        U1[0, x] = P1_16
    g1 = face(G1, 2), face(G1, 3), face(G1, 4)
    even_v, odd_v = U1.at[0], U1.at[1]
    weight1 = G1.at[1]
    sweep(even_v, odd_v, g1, face(G1, 0), weight1, 1, 13)
    sweep(odd_v, even_v, g1, face(G1, 0), weight1, 2, 12)
    sweep(even_v, odd_v, g1, face(G1, 0), weight1, 3, 11)

    lifted = [finer(odd_v[5 + x], 4) for x in range(-2, 6)]
    for x in range(X0):
        for part in (E, O):
            VA[x, :, part] = VP[x, :, part] + lifted[(x - 3) // 2 + 2]
    sweep0(VA, VB, 1, X0 - 1)
    sweep0(VB, VA, 2, X0 - 2)
    is_even = lax.rem(lane, 2) == 0
    for x in range(8):
        halves = []
        for v, total, part in couplings0(VA, H0 + x):
            result = 0.2 * v[0:8] + W0[H0 + x, own, part] * (F0[0, H0 + x, own, part] + total[0:8])
            halves.append(result)
        for part, index in ((E, half_lanes), (O, half_lanes + 64)):
            out[x, :, part] = jnp.where(is_even, pick(halves[0], index, 1), pick(halves[1], index, 1))

    near3y.sent(dummy)
    near2x.sent(dummy)


def solution(mesh):
    nx, ny = mesh.shape["bx"], mesh.shape["by"]

    def vmem(*shape):
        return pltpu.VMEM(shape, F32)

    def body(*args):
        return pl.pallas_call(
            functools.partial(kernel, nx, ny),
            out_shape=pltpu.VMEM((8, 8, 256), F32),
            in_specs=[pl.BlockSpec(memory_space=pltpu.HBM)] * 5,
            out_specs=pl.BlockSpec(memory_space=pltpu.VMEM),
            scratch_shapes=[
                vmem(5, 8, 8, 256), pltpu.SemaphoreType.DMA((5,)),
                vmem(5, X0 + 1, 16, 256), vmem(8, 8, 256), vmem(8, 8, 256), vmem(8, 256), vmem(8, 8, 256),
                vmem(8, 8, 256), vmem(8, 8, 256), vmem(X0, 16, 256), vmem(X0, 16, 256), vmem(X0, 16, 256), vmem(X0, 16, 256),
                vmem(5, X1 + 1, 24, 128), vmem(X1, 24, 128), vmem(X1, 24, 128), vmem(X1, 24, 128), vmem(X1, 24, 128),
                vmem(6, 14, 16, 128), vmem(2, 14, 16, 128),
                vmem(6, X2, 16, 128), vmem(2, X2, 16, 128), vmem(X2, 16, 128), vmem(X2, 16, 128), vmem(8, 16, 128), vmem(X2, 16, 128), vmem(X2, 16, 128),
                vmem(SLOTS, 1, 128), vmem(4, SLOTS, 1, 128), vmem(GROUPS, 8, 128), vmem(4, GROUPS, 8, 128),
                vmem(5, GROUPS, 16, 128), vmem(GROUPS, 16, 128), vmem(GROUPS, 16, 128), vmem(GROUPS, 16, 128),
                vmem(8192, 128),
                pltpu.SemaphoreType.DMA((16,)), pltpu.SemaphoreType.DMA((16,)),
            ],
            compiler_params=pltpu.CompilerParams(
                collective_id=0, has_side_effects=True, vmem_limit_bytes=60 * 2**20
            ),
        )(*args)

    return jax.shard_map(
        body,
        mesh=mesh,
        in_specs=(P("bx", "by", None),) * 5,
        out_specs=P("bx", "by", None),
        check_vma=False,
    )
```

```python
import functools

import jax
import jax.numpy as jnp
from jax import lax
from jax.experimental import pallas as pl
from jax.experimental.pallas import tpu as pltpu
from jax.sharding import PartitionSpec as P

MESH = pl.DeviceIdType.MESH
F32 = jnp.float32
COARSE = 8

H0, H1, H2, H3 = 3, 9, 6, 10
X0, X1, X2 = 8 + 2 * H0, 4 + 2 * H1, 2 + 2 * H2
SLOTS, GROUPS = 2 * H3 + 1, (2 * H3 + 4) // 4


def reach(offset, size, halo):
    if offset == 0:
        return 0, size
    near = size * (abs(offset) - 1)
    count = min(size, halo - near)
    if count <= 0:
        return 0, 0
    return (0, count) if offset > 0 else (size - count, count)


def gap(offset, size):
    return 0 if offset == 0 else size * (abs(offset) - 1) + 1


def distance(offset):
    dx, dy = abs(offset[0]), offset[1] % 16
    return dx / 2 + min(dy % 4, 4 - dy % 4) + min(dy / 4, 4 - dy / 4)


def farthest_first(offsets):
    return sorted(offsets, key=distance, reverse=True)


AROUND = farthest_first([(a, b) for a in (-1, 0, 1) for b in (-1, 0, 1) if (a, b) != (0, 0)])
WIDE = farthest_first(
    [
        (a, b)
        for a in range(-3, 4)
        for b in range(-3, 4)
        if (a, b) != (0, 0) and gap(a, 4) + gap(b, 4) <= H1
    ]
)
ALONG_X = [dx for dx, _ in farthest_first([(a, 0) for a in range(-H3, H3 + 1) if a])]
ALONG_Y = [dy for _, dy in farthest_first([(0, b) for b in range(1, 16)])]
NEAR = [-2, 2, -3, 3, -1, 1]
PARTNERS = farthest_first(
    sorted(set(WIDE) | {(a, 0) for a in ALONG_X} | {(0, b if b <= 8 else b - 16) for b in ALONG_Y})
)[::-1]


def lanes(shape=(8, 128)):
    return lax.broadcasted_iota(jnp.int32, shape, 1)


def rows(shape=(8, 128)):
    return lax.broadcasted_iota(jnp.int32, shape, 0)


def pick(tile, index, axis):
    return jnp.take_along_axis(tile, index, axis=axis, mode="promise_in_bounds")


def up(value):
    return pltpu.roll(value, value.shape[0] - 1, 0)


def down(value):
    return pltpu.roll(value, 1, 0)


def right(value):
    return pltpu.roll(value, 127, 1)


def left(value):
    return pltpu.roll(value, 1, 1)


def coarsen(planes, kind, lane_index=None):
    out = []
    for i in range(0, len(planes), 2):
        total = planes[i] if kind == "x" else planes[i] + planes[i + 1]
        if kind != "y":
            total = total + up(total)
        total = pick(total, lax.rem(2 * rows(), 8), 0)
        if lane_index is not None:
            if kind != "z":
                total = total + right(total)
            total = pick(total, lane_index, 1)
        out.append(total * (0.125 if kind == "c" else 0.0625))
    return out


def couplings(get, bx, by, bz, x):
    v = get(x)
    cy, cz = by(x), bz(x)
    total = bx(x) * get(x - 1) + bx(x + 1) * get(x + 1)
    total = total + cy * down(v) + up(cy * v)
    return v, total + cz * left(v) + right(cz * v)


class Copies:
    def __init__(self, place, send_sems, recv_sems, number):
        self.place, self.number = place, number
        self.send_sem, self.recv_sem = send_sems.at[number], recv_sems.at[number]
        self.count = 0

    def start(self, source, target, offset):
        pltpu.make_async_remote_copy(
            src_ref=source,
            dst_ref=target,
            send_sem=self.send_sem,
            recv_sem=self.recv_sem,
            device_id=self.place(offset),
            device_id_type=MESH,
        ).start()
        size = 1
        for dim in source.shape:
            size *= dim
        self.count += size // 128

    def _wait(self, sem, dummy):
        part = dummy.at[pl.ds(0, self.count)]
        pltpu.make_async_copy(part, part, sem).wait()

    def arrived(self, dummy):
        self._wait(self.recv_sem, dummy)

    def sent(self, dummy):
        self._wait(self.send_sem, dummy)


def kernel(nx, ny, rhs, acoef, beta_x, beta_y, beta_z, out,
           IN, in_sems, F0, A0, E0, HX, HY, D0, G0, W0, VA, VB, VP,
           F1, D1, W1, P1, Q1, G1, U1,
           F2, S2, T2, W2, FP, P2, Q2,
           R3, RC, PK, PC, F3, W3, P3, Q3,
           dummy, send_sems, recv_sems):
    ix, iy = lax.axis_index("bx"), lax.axis_index("by")
    loads = [
        pltpu.make_async_copy(ref, IN.at[number], in_sems.at[number])
        for number, ref in enumerate((beta_x, beta_y, beta_z, acoef, rhs))
    ]
    for load in loads:
        load.start()

    def place(offset):
        return (lax.rem(ix + (offset[0] % nx), nx), lax.rem(iy + (offset[1] % ny), ny))

    def group(number):
        return Copies(place, send_sems, recv_sems, number)

    barrier = pltpu.get_barrier_semaphore()
    for offset in PARTNERS:
        pl.semaphore_signal(barrier, inc=1, device_id=place(offset), device_id_type=MESH)

    lane, row = lanes(), rows()
    even = lax.rem(2 * lane, 128)
    keep_x = jnp.where(ix == 0, 0.0, 1.0).astype(F32)
    keep_y = jnp.where(iy == 0, 0.0, 1.0).astype(F32)
    keep_rows = jnp.where(row == 0, keep_y, 1.0)
    E, O = pl.ds(0, 128), pl.ds(128, 128)

    def split(number, x):
        low, high = IN[number, x, :, E], IN[number, x, :, O]
        return tuple(
            jnp.where(lane < 64, pick(low, even + odd, 1), pick(high, even + odd, 1)) for odd in (0, 1)
        )

    own = pl.ds(0, 8)
    for load in loads:
        load.wait()
    for x in range(8):
        px = H0 + x
        bx, by, bz, a, f = (split(number, x) for number in range(5))
        for half, part in ((0, E), (1, O)):
            bxm = bx[half] * keep_x if x == 0 else bx[half]
            bym = by[half] * keep_rows
            extra = by[half] - bym
            if x == 0:
                extra = extra + (bx[half] - bxm)
            bzm = bz[half]
            if half == 0:
                bzm = jnp.where(lane == 0, 0.0, bzm)
                extra = extra + (bz[half] - bzm)
            F0[0, px, own, part] = f[half]
            F0[1, px, own, part] = a[half] + extra
            F0[2, px, own, part] = bxm
            F0[3, px, own, part] = bym
            F0[4, px, own, part] = bzm
            A0[x, :, part] = a[half]
            E0[x, :, part] = extra

    for x in range(8):
        for half, part in ((0, E), (1, O)):
            bx, by, bz = (F0[n, H0 + x, own, part] for n in (2, 3, 4))
            total = F0[1, H0 + x, own, part] + bx + by + up(by) + bz
            if x < 7:
                total = total + F0[2, H0 + x + 1, own, part]
            D0[x, :, part] = total + (F0[4, H0 + x, own, O] if half == 0 else right(F0[4, H0 + x, own, E]))

    def both(get):
        return [get(x, E) + get(x, O) for x in range(8)]

    to64, to32 = even, lax.rem(2 * lane, 64)
    a1 = coarsen(both(lambda x, p: A0[x, :, p]), "c")
    e1 = [0.5 * t for t in coarsen(both(lambda x, p: E0[x, :, p]), "c")]
    bx1 = coarsen(both(lambda x, p: F0[2, H0 + x, own, p]), "x")
    by1 = coarsen(both(lambda x, p: F0[3, H0 + x, own, p]), "y")
    bz1 = coarsen([F0[4, H0 + x, own, E] for x in range(8)], "z")
    a2 = coarsen(a1, "c", to64)
    e2 = [0.5 * t for t in coarsen(e1, "c", to64)]
    bx2, by2, bz2 = coarsen(bx1, "x", to64), coarsen(by1, "y", to64), coarsen(bz1, "z", to64)
    a3 = coarsen(a2, "c", to32)
    e3 = [0.5 * t for t in coarsen(e2, "c", to32)]
    bx3, by3, bz3 = coarsen(bx2, "x", to32), coarsen(by2, "y", to32), coarsen(bz2, "z", to32)

    for number, field in enumerate(([a + e for a, e in zip(a1, e1)], bx1, by1, bz1)):
        for i in range(4):
            F1[1 + number, H1 + i, pl.ds(0, 4)] = field[i][0:4]

    def wide_spans(dx, dy, more=0):
        fx, cx = reach(-dx, 4, H1 + (more if dx < 0 else 0))
        fy, cy = reach(-dy, 4, H1 + (more if dy < 0 else 0))
        return pl.ds(H1 + fx, cx), pl.ds(fy, cy), pl.ds(H1 - 4 * dx + fx, cx), pl.ds((fy - 4 * dy) % 24, cy)

    def send1(offset, collection):
        sx, sy, tx, ty = wide_spans(*offset, 1)
        collection.start(F1.at[pl.ds(1, 4), sx, sy], F1.at[pl.ds(1, 4), tx, ty], offset)

    pl.semaphore_wait(barrier, len(PARTNERS))

    faces = group(0)
    faces.start(F0.at[2, H0, own], HX.at[:, :], (-1, 0))
    faces.start(F0.at[3, pl.ds(H0, 8), pl.ds(0, 1)], HY.at[:, pl.ds(0, 1)], (0, -1))
    coef1y = group(2)
    for dy in NEAR:
        send1((0, dy), coef1y)
    halo = group(1)

    def span_x(offset, wide):
        if offset == 0:
            return pl.ds(H0, 8), pl.ds(H0, 8)
        if offset < 0:
            return pl.ds(H0, wide), pl.ds(H0 + 8, wide)
        return pl.ds(H0 + 8 - wide, wide), pl.ds(H0 - wide, wide)

    def span_y(offset, wide):
        if offset == 0:
            return pl.ds(0, 8), pl.ds(0, 8)
        if offset < 0:
            return pl.ds(0, wide), pl.ds(8, wide)
        return pl.ds(8 - wide, wide), pl.ds(16 - wide, wide)

    def spans(dx, dy):
        width = 2 if dx != 0 and dy != 0 else 3
        sx, tx = span_x(dx, width)
        sy, ty = span_y(dy, width)
        return sx, sy, tx, ty

    for dx, dy, number, x, y in (
        (-1, -1, 2, 2, 0), (-1, -1, 3, 2, 0), (-1, -1, 2, 0, 2), (-1, -1, 3, 0, 2),
        (-1, 1, 2, 2, 7), (-1, 1, 2, 0, 5), (1, -1, 3, 7, 2), (1, -1, 3, 5, 0),
    ):
        source = F0.at[number, H0 + x, pl.ds(y, 1)]
        halo.start(source, F0.at[number, H0 + x - 8 * dx, pl.ds((y - 8 * dy) % 16, 1)], (dx, dy))
    for dx, dy in AROUND:
        if dx and dy:
            sx, sy, tx, ty = spans(dx, dy)
            halo.start(F0.at[:, sx, sy], F0.at[:, tx, ty], (dx, dy))
    planes = pl.ds(H0, 8)
    for dy in (-1, 1):
        near, far, there, beyond = (0, 2, 8, 10) if dy < 0 else (6, 5, 14, 13)
        halo.start(F0.at[:, planes, pl.ds(near, 2)], F0.at[:, planes, pl.ds(there, 2)], (0, dy))
        halo.start(F0.at[0, planes, pl.ds(far, 1)], F0.at[0, planes, pl.ds(beyond, 1)], (0, dy))
        halo.start(D0.at[:, pl.ds(far, 1)], F0.at[1, planes, pl.ds(beyond, 1)], (0, dy))
        if dy < 0:
            halo.start(F0.at[3, planes, pl.ds(far, 1)], F0.at[3, planes, pl.ds(beyond, 1)], (0, dy))
    for dx in (-1, 1):
        sx, sy, tx, ty = spans(dx, 0)
        halo.start(F0.at[:, sx, sy], F0.at[:, tx, ty], (dx, 0))
    halo.start(F0.at[2, H0 + 3, own], F0.at[2, H0 + 11, own], (-1, 0))

    coef1x = group(4)
    for dx in NEAR:
        send1((dx, 0), coef1x)

    faces.arrived(dummy)
    hx = HX[:, E] + HX[:, O]
    hx1 = coarsen([hx, hx], "x")[0]
    hx2 = coarsen([hx1, hx1], "x", to64)[0]
    hx3 = coarsen([hx2, hx2], "x", to32)[0]
    hy = [HY[x, :, E] + HY[x, :, O] for x in range(8)]
    hy1 = [0.0625 * (hy[2 * i] + hy[2 * i + 1]) for i in range(4)]

    def squeeze(t, index):
        return pick(t + right(t), index, 1) * 0.0625

    hy2 = [squeeze(hy1[2 * i] + hy1[2 * i + 1], to64) for i in range(2)]
    hy3 = squeeze(hy2[0] + hy2[1], to32)

    def diag_of(a, e, bx, by, bz, hx_plane, hy_rows, last):
        result = []
        for i in range(len(a)):
            high_x = bx[i + 1] if i + 1 < len(a) else hx_plane
            edge = pltpu.roll(hy_rows[i], last, 0) if last else hy_rows[i]
            high_y = jnp.where(row == last, edge, up(by[i]))
            result.append(a[i] + e[i] + bx[i] + high_x + by[i] + high_y + bz[i] + right(bz[i]))
        return result

    d2 = diag_of(a2, e2, bx2, by2, bz2, hx2, hy2, 1)
    d3 = diag_of(a3, e3, bx3, by3, bz3, hx3, [hy3], 0)
    two = pl.ds(0, 2)
    mid = pl.ds(H2, 2)
    for i in range(2):
        own2 = [jnp.where(lane < 64, a, b) for a, b in ((d2[i], bx2[i]), (by2[i], bz2[i]))]
        for number in range(2):
            S2[number, H2 + i, two] = own2[number][0:2]
    for number, field in enumerate((d3, bx3, by3, bz3)):
        RC[number, H3] = field[0][0:1]

    coef2y = group(6)
    for dy in NEAR:
        coef2y.start(S2.at[:, mid, two], S2.at[:, mid, pl.ds((-2 * dy) % 16, 2)], (0, dy))
    coef1y.arrived(dummy)
    corner1x = group(5)
    for dx, parts in (
        (-2, ((0, 4, 4, 4), (0, 4, 19, 5), (0, 1, 8, 1))),
        (2, ((0, 4, 4, 4), (0, 4, 20, 4), (3, 1, 8, 1))),
        (-1, ((0, 4, 4, 4), (0, 4, 8, 5), (0, 4, 16, 8), (0, 1, 15, 1))),
        (1, ((0, 4, 4, 4), (0, 4, 8, 5), (0, 4, 16, 8))),
        (-3, ((0, 1, 4, 1), (0, 1, 23, 1))),
        (3, ((3, 1, 4, 1),)),
    ):
        for plane, planes_sent, first, count in parts:
            span = pl.ds(first, count)
            corner1x.start(
                F1.at[pl.ds(1, 4), pl.ds(H1 + plane, planes_sent), span],
                F1.at[pl.ds(1, 4), pl.ds(H1 + plane - 4 * dx, planes_sent), span],
                (dx, 0),
            )

    halo.arrived(dummy)
    for x in range(X0):
        hz = F0[4, x, :, E], F0[4, x, :, O]
        for half, part in ((0, E), (1, O)):
            by = F0[3, x, :, part]
            total = F0[1, x, :, part] + F0[2, x, :, part] + F0[2, x + 1, :, part] + by + up(by) + hz[half]
            total = total + (hz[1] if half == 0 else right(hz[0]))
            if H0 <= x < H0 + 8:
                known = F0[1, x, pl.ds(8, 8), part]
                if x == H0 + 7:
                    known = known + F0[2, x + 1, pl.ds(8, 8), part]
                outer = jnp.where((row == 2) | (row == 5), known, total[8:16])
                total = jnp.concatenate([total[0:8], outer], axis=0)
            w = 0.8 / total
            W0[x, :, part] = w
            VA[x, :, part] = w * F0[0, x, :, part]
            if H0 <= x < H0 + 8:
                G0[x - H0, :, part] = total[0:8]

    def couplings0(src, x, count=16):
        ve, vo = src[x, :, E], src[x, :, O]
        ze, zo = F0[4, x, :, E], F0[4, x, :, O]
        sums = []
        for v, part in ((ve, E), (vo, O)):
            by = F0[3, x, :, part]
            total = F0[2, x, :, part] * src[x - 1, :, part] + F0[2, x + 1, :, part] * src[x + 1, :, part]
            sums.append(total + by * down(v) + up(by * v))
        sums[0] = sums[0] + ze * left(vo) + zo * vo
        sums[1] = sums[1] + zo * ve + right(ze * ve)
        return ((ve, sums[0], E), (vo, sums[1], O))

    def sweep0(src, dst, first, last):
        for x in range(first, last):
            for v, total, part in couplings0(src, x):
                dst[x, :, part] = 0.2 * v + W0[x, :, part] * (F0[0, x, :, part] + total)

    sweep0(VA, VB, 1, X0 - 1)
    sweep0(VB, VA, 2, X0 - 2)
    remains = []
    for x in range(8):
        parts = []
        for v, total, part in couplings0(VA, H0 + x):
            v, total = v[0:8], total[0:8]
            parts.append(F0[0, H0 + x, own, part] + total - G0[x, :, part] * v)
            VP[H0 + x, own, part] = v
        remains.append(parts[0] + parts[1])
    f1 = coarsen(remains, "c")
    for i in range(4):
        F1[0, H1 + i, pl.ds(0, 4)] = f1[i][0:4]

    wide_f = group(9)
    for offset in WIDE:
        sx, sy, tx, ty = wide_spans(*offset)
        wide_f.start(F1.at[0, sx, sy], F1.at[0, tx, ty], offset)

    def along_x2(collection, ref, lead):
        for dx in NEAR:
            for first, count in {1: ((0, 8), (10, 6)), 2: ((0, 5), (13, 3)), 3: ((0, 3), (15, 1))}[abs(dx)]:
                source = ref.at[(*lead, mid, pl.ds(first, count))]
                collection.start(source, ref.at[(*lead, pl.ds(H2 - 2 * dx, 2), pl.ds(first, count))], (dx, 0))

    coef2y.arrived(dummy)
    coef2x = group(7)
    along_x2(coef2x, S2, (slice(None),))
    coef3x = group(8)
    for dx in ALONG_X:
        coef3x.start(RC.at[:, H3], RC.at[:, H3 - dx], (dx, 0))

    def packed(get):
        result = []
        for g in range(GROUPS):
            columns = [get(min(4 * g + k, SLOTS - 1)) for k in range(4)]
            line = lane[0:1]
            result.append(
                jnp.where(
                    line < 64,
                    jnp.where(line < 32, columns[0], columns[1]),
                    jnp.where(line < 96, columns[2], columns[3]),
                )
            )
        return result

    one = pl.ds(0, 1)
    coef1x.arrived(dummy)
    corner1x.arrived(dummy)
    for x in range(X1):
        by, bz = F1[3, x], F1[4, x]
        total = F1[1, x] + F1[2, x] + F1[2, x + 1] + by + up(by) + bz + right(bz)
        D1[x] = total
        W1[x] = 0.8 / total
    coef2x.arrived(dummy)
    wide_lanes = lanes((16, 128))

    def unpacked(value):
        swapped = pltpu.roll(value, 64, 1)
        return jnp.where(wide_lanes < 64, value, swapped), jnp.where(wide_lanes < 64, swapped, value)

    for x in range(X2):
        F2[2, x], F2[3, x] = unpacked(S2[0, x])
        F2[4, x], F2[5, x] = unpacked(S2[1, x])
        W2[x] = 0.8 / F2[2, x]

    def face(ref, number):
        return lambda x: ref[number, x]

    def sweep(src, dst, coeffs, source, weight, first, last, shift=0):
        for x in range(first, last):
            v, total = couplings(lambda p: src[p - shift], *coeffs, x)
            dst[x - shift] = 0.2 * v + weight[x] * (source(x) + total)

    c1 = face(F1, 2), face(F1, 3), face(F1, 4)
    wide_f.arrived(dummy)
    for x in range(X1):
        P1[x] = W1[x] * F1[0, x]
    sweep(P1, Q1, c1, face(F1, 0), W1, 1, X1 - 1)
    sweep(Q1, P1, c1, face(F1, 0), W1, 2, X1 - 2)

    def remains1(x):
        v, total = couplings(lambda p: P1[p], *c1, x)
        return F1[0, x] + total - D1[x] * v

    pairs = lax.rem(2 * row, 8)
    for i in range(8):
        x = H1 - 6 + 2 * i
        total = remains1(x) + remains1(x + 1)
        tiles = []
        for t in range(3):
            tile = total[8 * t : 8 * t + 8]
            tiles.append(pick(tile + up(tile), pairs, 0))
        tiles = [jnp.where(row < 4, tiles[0], tiles[1]), tiles[2]]
        tiles = [pick(tile + right(tile), to64, 1) * 0.125 for tile in tiles]
        FP[i] = jnp.concatenate(tiles, axis=0)

    c2 = face(F2, 3), face(F2, 4), face(F2, 5)
    for i in range(8):
        P2[i] = W2[i + 3] * FP[i]
    sweep(P2, Q2, c2, lambda x: FP[x - 3], W2, 4, 10, 3)
    sweep(Q2, P2, c2, lambda x: FP[x - 3], W2, 5, 9, 3)
    total = None
    for x in (6, 7):
        v, s = couplings(lambda p: P2[p - 3], *c2, x)
        rest = (FP[x - 3] + s - F2[2, x] * v)[0:8]
        total = rest if total is None else total + rest
        T2[x, two] = jnp.where(lane < 64, FP[x - 3][0:8], v[0:8])[0:2]
    total = total + up(total)
    f3 = (pick(total + right(total), to32, 1) * 0.125)[0:1]
    R3[H3] = f3

    near3x = group(10)
    for dx in ALONG_X:
        near3x.start(R3.at[H3], R3.at[H3 - dx], (dx, 0))
    near2y = group(11)
    for dy in NEAR:
        near2y.start(T2.at[mid, two], T2.at[mid, pl.ds((-2 * dy) % 16, 2)], (0, dy))
    coef3x.arrived(dummy)
    for number in range(4):
        for g, value in enumerate(packed(lambda s: RC[number, s])):
            PC[number, g, one] = value
            F3[1 + number, g, one] = value
    coef3y = group(13)
    for dy in ALONG_Y:
        coef3y.start(PC.at[:, :, one], F3.at[pl.ds(1, 4), :, pl.ds(16 - dy, 1)], (0, dy))
    halo_v = group(12)
    for dx, dy in AROUND:
        sx, sy, tx, ty = spans(dx, dy)
        halo_v.start(VP.at[sx, sy], VP.at[tx, ty], (dx, dy))

    for x in range(14):
        p = H1 - 5 + x
        for number, get in enumerate((face(F1, 0), lambda q: W1[q], face(F1, 2), face(F1, 3), face(F1, 4), lambda q: P1[q])):
            value = get(p)
            mixed = jnp.where(row < 3, value[8:16], value[16:24])
            G1[number, x] = jnp.concatenate([value[0:8], mixed], axis=0)
    near3x.arrived(dummy)
    for g, value in enumerate(packed(lambda s: R3[s])):
        PK[g, one] = value
        F3[0, g, one] = value
    near3y = group(14)
    for dy in ALONG_Y:
        near3y.start(PK.at[:, one], F3.at[0, :, pl.ds(16 - dy, 1)], (0, dy))
    near2y.arrived(dummy)
    near2x = group(15)
    along_x2(near2x, T2, ())
    coef3y.arrived(dummy)
    for g in range(GROUPS):
        W3[g] = 0.8 / F3[1, g]
    halo_v.arrived(dummy)
    for done in (faces, halo, coef1y, coef1x, coef2y, coef3x, wide_f, corner1x, coef2x, near3x, near2y, coef3y, halo_v):
        done.sent(dummy)

    near3y.arrived(dummy)
    line = lanes((16, 128))
    for g in range(GROUPS):
        P3[g] = W3[g] * F3[0, g]
    src, dst = P3, Q3
    for step in range(COARSE - 1):
        for g in range(GROUPS):
            v, cx, cy, cz = src[g], F3[2, g], F3[3, g], F3[4, g]
            ahead = min(g + 1, GROUPS - 1)
            low = jnp.where(line < 32, pltpu.roll(src[max(g - 1, 0)], 32, 1), pltpu.roll(v, 32, 1))
            high = jnp.where(
                line >= 96, pltpu.roll(F3[2, ahead] * src[ahead], 96, 1), pltpu.roll(cx * v, 96, 1)
            )
            total = cx * low + high + cy * down(v) + up(cy * v) + cz * left(v) + right(cz * v)
            dst[g] = 0.2 * v + W3[g] * (F3[0, g] + total)
        src, dst = dst, src

    half_rows = lax.shift_right_logical(row, 1)

    def onto2(x):
        slot = H3 + x
        index = 32 * (slot % 4) + lax.shift_right_logical(lax.rem(lane, 64), 1)
        value = src[slot // 4]
        low, high = (pick(value[8 * t : 8 * t + 8], index, 1) for t in (0, 1))
        return jnp.concatenate([pick(low, half_rows, 0), pick(high, half_rows + 4, 0)], axis=0)

    lifted = [onto2(x) for x in range(-3, 4)]
    near2x.arrived(dummy)
    for x in range(X2):
        F2[0, x], value = unpacked(T2[x])
        P2[x] = value + lifted[x // 2]
    sweep(P2, Q2, c2, face(F2, 0), W2, 1, X2 - 1)
    sweep(Q2, P2, c2, face(F2, 0), W2, 2, X2 - 2)
    sweep(P2, Q2, c2, face(F2, 0), W2, 3, X2 - 3)

    half_lanes = lax.shift_right_logical(lane, 1)

    def finer(value, limit, lane_index=None):
        tiles = [value[0:8], value[8:16]]
        if lane_index is not None:
            tiles = [pick(tile, lane_index, 1) for tile in tiles]
        upper = jnp.where(row < limit, pick(tiles[0], half_rows + 4, 0), pick(tiles[1], half_rows + 4, 0))
        return jnp.concatenate([pick(tiles[0], half_rows, 0), upper], axis=0)

    lifted = [finer(Q2[H2 + x], 3, half_lanes) for x in range(-3, 5)]
    for x in range(14):
        P1_16 = G1[5, x] + lifted[(x - 5) // 2 + 3]
        U1[0, x] = P1_16
    g1 = face(G1, 2), face(G1, 3), face(G1, 4)
    even_v, odd_v = U1.at[0], U1.at[1]
    weight1 = G1.at[1]
    sweep(even_v, odd_v, g1, face(G1, 0), weight1, 1, 13)
    sweep(odd_v, even_v, g1, face(G1, 0), weight1, 2, 12)
    sweep(even_v, odd_v, g1, face(G1, 0), weight1, 3, 11)

    lifted = [finer(odd_v[5 + x], 4) for x in range(-2, 6)]
    for x in range(X0):
        for part in (E, O):
            VA[x, :, part] = VP[x, :, part] + lifted[(x - 3) // 2 + 2]
    sweep0(VA, VB, 1, X0 - 1)
    sweep0(VB, VA, 2, X0 - 2)
    is_even = lax.rem(lane, 2) == 0
    for x in range(8):
        halves = []
        for v, total, part in couplings0(VA, H0 + x):
            result = 0.2 * v[0:8] + W0[H0 + x, own, part] * (F0[0, H0 + x, own, part] + total[0:8])
            halves.append(result)
        for part, index in ((E, half_lanes), (O, half_lanes + 64)):
            out[x, :, part] = jnp.where(is_even, pick(halves[0], index, 1), pick(halves[1], index, 1))

    near3y.sent(dummy)
    near2x.sent(dummy)


def solution(mesh):
    nx, ny = mesh.shape["bx"], mesh.shape["by"]

    def vmem(*shape):
        return pltpu.VMEM(shape, F32)

    def body(*args):
        return pl.pallas_call(
            functools.partial(kernel, nx, ny),
            out_shape=pltpu.VMEM((8, 8, 256), F32),
            in_specs=[pl.BlockSpec(memory_space=pltpu.HBM)] * 5,
            out_specs=pl.BlockSpec(memory_space=pltpu.VMEM),
            scratch_shapes=[
                vmem(5, 8, 8, 256), pltpu.SemaphoreType.DMA((5,)),
                vmem(5, X0 + 1, 16, 256), vmem(8, 8, 256), vmem(8, 8, 256), vmem(8, 256), vmem(8, 8, 256),
                vmem(8, 8, 256), vmem(8, 8, 256), vmem(X0, 16, 256), vmem(X0, 16, 256), vmem(X0, 16, 256), vmem(X0, 16, 256),
                vmem(5, X1 + 1, 24, 128), vmem(X1, 24, 128), vmem(X1, 24, 128), vmem(X1, 24, 128), vmem(X1, 24, 128),
                vmem(6, 14, 16, 128), vmem(2, 14, 16, 128),
                vmem(6, X2, 16, 128), vmem(2, X2, 16, 128), vmem(X2, 16, 128), vmem(X2, 16, 128), vmem(8, 16, 128), vmem(X2, 16, 128), vmem(X2, 16, 128),
                vmem(SLOTS, 1, 128), vmem(4, SLOTS, 1, 128), vmem(GROUPS, 8, 128), vmem(4, GROUPS, 8, 128),
                vmem(5, GROUPS, 16, 128), vmem(GROUPS, 16, 128), vmem(GROUPS, 16, 128), vmem(GROUPS, 16, 128),
                vmem(8192, 128),
                pltpu.SemaphoreType.DMA((16,)), pltpu.SemaphoreType.DMA((16,)),
            ],
            compiler_params=pltpu.CompilerParams(
                collective_id=0, has_side_effects=True, vmem_limit_bytes=60 * 2**20
            ),
        )(*args)

    return jax.shard_map(
        body,
        mesh=mesh,
        in_specs=(P("bx", "by", None),) * 5,
        out_specs=P("bx", "by", None),
        check_vma=False,
    )
```
